32 devices in a mesh: dom: 32 (over z, y, x, core).
Axes of the slice: x: 2, y: 2, z: 4, core: 2. Of those that a mesh axis runs over, the one named last changes fastest.
Arguments:
- features: bfloat16 [16384, 256], P('dom'), may hold values from -20 to 20, as said below
- w_self: bfloat16 [256, 256], replicated, may hold values from -0.375 to 0.375
- w_neigh: bfloat16 [256, 256], replicated, may hold values from -0.375 to 0.375
- neighbors: int32 [16384, 10], P('dom'), may hold values from 0 to 1151
- degree: int32 [16384], P('dom'), may hold values from 1 to 10
- boundary: int32 [32, 5, 128], P('dom'), may hold values from 0 to 511
- upstream: bfloat16 [16384, 256], P('dom'), may hold values from -6 to 6
Outputs:
- hidden: bfloat16 [16384, 256], P('dom')
- node_grad: bfloat16 [16384, 256], P('dom')
- weight_step: float32 [512, 256], replicated
The draws below stay inside these ranges and needn't reach their ends.
Inputs may be any that keep to these rules, and one draw needn't show every extreme that they name: `features`: feature values lie in the stated range.
All inputs are finite; a program needn't handle non-finite values.
Results may differ from the reference program's by a relative error of at most 0.006.
Values may be sent and summed in bfloat16 or wider, within the bound.
A program may use at most 64 MiB of HBM per device.

```python
import jax
import jax.numpy as jnp
from jax import lax

D = 256
NODE_DEV = 512
BND = 128
DEG = 10
LEVELS = 5
NODES = 16384
N_DOM = 32


def draw_features(key, part):
    key = jax.random.fold_in(key, 11)
    key_values, key_columns = jax.random.split(key, 2)
    ramp = 3.0 ** (jnp.arange(D, dtype=jnp.float32) / D)
    column_scale = ramp * jnp.exp(jax.random.uniform(key_columns, (D,), jnp.float32, -0.5, 0.5))
    values = jax.random.truncated_normal(key_values, -4.0, 4.0, (NODES, D), jnp.float32)
    return (values * column_scale[None, :]).astype(jnp.bfloat16)


def set_ends(values, rng, least, top_value):
    longest = values.shape.index(max(values.shape))
    spots = []
    for shift in (0, 1):
        where = [jax.random.randint(jax.random.fold_in(rng, axis), (), 0, length) for axis, length in enumerate(values.shape)]
        where[longest] = (where[longest] + shift) % values.shape[longest]
        spots.append(tuple(where))
    return values.at[spots[0]].set(least).at[spots[1]].set(top_value)


def block_scale(stream_key, extent, cuts, low, largest):
    def one(axis_at, shards_of):
        draws = jax.random.uniform(jax.random.fold_in(jax.random.fold_in(stream_key, 6), axis_at), (shards_of,), jnp.float32, low / len(cuts), largest / len(cuts))
        return jnp.repeat(jnp.exp(draws), extent[axis_at] // shards_of).reshape((-1,) + (1,) * (len(extent) - axis_at - 1))

    loudness = one(*cuts[0])
    for cut in cuts[1:]:
        loudness = loudness * one(*cut)
    return loudness


def bell_draw(key, extent, scale, reach, shards=(), held_as=jnp.bfloat16):
    values = scale * jax.random.normal(key, extent, jnp.float32)
    if shards:
        values = values * block_scale(key, extent, shards, -0.22, 0.18)
    return jnp.clip(values, -reach, reach).astype(held_as)


def setup_inputs(seed: int = 0) -> dict:
    seeds = jax.random.split(jax.random.key(seed), 8)
    features = draw_features(jax.random.fold_in(seeds[7], 71), 0)
    w_self = bell_draw(seeds[1], (D, D), D ** -0.5, 0.375)
    w_neigh = bell_draw(seeds[2], (D, D), D ** -0.5, 0.375)
    neighbors = set_ends(jax.random.randint(seeds[3], (NODES, DEG), 0, NODE_DEV + LEVELS * BND), jax.random.fold_in(seeds[3], 1), 0, (NODE_DEV + LEVELS * BND) - 1).astype(jnp.int32)
    degree = set_ends(jax.random.randint(seeds[4], (NODES,), 1, DEG + 1), jax.random.fold_in(seeds[4], 1), 1, DEG).astype(jnp.int32)
    boundary = set_ends(jax.random.randint(seeds[5], (N_DOM, LEVELS, BND), 0, NODE_DEV), jax.random.fold_in(seeds[5], 1), 0, NODE_DEV - 1).astype(jnp.int32)
    upstream = bell_draw(seeds[6], (NODES, D), 1.0, 6.0, ((0, 32),))
    return dict(features=features, w_self=w_self, w_neigh=w_neigh, neighbors=neighbors, degree=degree, boundary=boundary, upstream=upstream)


epsilon = 1e-06

def aggregate(packed):
    block, remote, slot_index, degree_int = packed
    extended = jnp.concatenate([block, remote.reshape(LEVELS * BND, D)], axis=0)
    summed = jnp.zeros((NODE_DEV, D), jnp.float32)
    for slot in range(DEG):
        usable = (slot < degree_int)[:, None]
        summed = summed + jnp.where(usable, extended[slot_index[:, slot]].astype(jnp.float32), jnp.float32(0.0))
    return (summed / degree_int.astype(jnp.float32)[:, None]).astype(jnp.bfloat16)

def spread(packed):
    slot_share, slot_index, degree_int = packed
    ext_grad = jnp.zeros((NODE_DEV + LEVELS * BND, D), jnp.float32)
    for slot in range(DEG):
        usable = (slot < degree_int)[:, None]
        ext_grad = ext_grad.at[slot_index[:, slot]].add(jnp.where(usable, slot_share, jnp.float32(0.0)))
    return (ext_grad[:NODE_DEV], ext_grad[NODE_DEV:].reshape(LEVELS, BND, D))

def collect(packed):
    local_part, returned, chosen = packed
    return local_part.at[chosen.reshape(-1)].add(returned.reshape(LEVELS * BND, D))

def reference(features, w_self, w_neigh, neighbors, degree, boundary, upstream):
    blocks = features.reshape(N_DOM, NODE_DEV, D)
    device_ids = jnp.arange(N_DOM, dtype=jnp.int32)
    level_ids = jnp.arange(LEVELS, dtype=jnp.int32)
    partner = jnp.bitwise_xor(device_ids[:, None], jnp.left_shift(jnp.int32(1), level_ids)[None, :])
    sent = jax.vmap(lambda block, chosen: block[chosen])(blocks, boundary)
    received = sent[partner, level_ids[None, :]]
    slot_blocks = neighbors.reshape(N_DOM, NODE_DEV, DEG)
    degree_blocks = degree.reshape(N_DOM, NODE_DEV)
    agg = lax.map(aggregate, (blocks, received, slot_blocks, degree_blocks)).reshape(NODES, D)
    pre_sum = jnp.dot(features, w_self, preferred_element_type=jnp.float32) + jnp.dot(agg, w_neigh, preferred_element_type=jnp.float32)
    hidden = jax.nn.silu(pre_sum).astype(jnp.bfloat16)
    sigmoid_pre = jax.nn.sigmoid(pre_sum)
    pre_grad = (upstream.astype(jnp.float32) * sigmoid_pre * (1.0 + pre_sum * (1.0 - sigmoid_pre))).astype(jnp.bfloat16)
    grad_self = jnp.dot(features.T, pre_grad, preferred_element_type=jnp.float32)
    grad_neigh = jnp.dot(agg.T, pre_grad, preferred_element_type=jnp.float32)
    stacked = jnp.concatenate([grad_self, grad_neigh], axis=0)
    weight_step = stacked * lax.rsqrt(jnp.mean(stacked * stacked) + epsilon)
    slot_share = jnp.dot(pre_grad, w_neigh.T, preferred_element_type=jnp.float32) / degree.astype(jnp.float32)[:, None]
    local_part, remote_part = lax.map(spread, (slot_share.reshape(N_DOM, NODE_DEV, D), slot_blocks, degree_blocks))
    returned = remote_part[partner, level_ids[None, :]]
    gathered = lax.map(collect, (local_part, returned, boundary)).reshape(NODES, D)
    node_grad = (jnp.dot(pre_grad, w_self.T, preferred_element_type=jnp.float32) + gathered).astype(jnp.bfloat16)
    return (hidden, node_grad, weight_step)
```

```python
import functools

import jax
import jax.numpy as jnp
from jax import lax
from jax.experimental import pallas as pl
from jax.experimental.pallas import tpu as pltpu
from jax.sharding import PartitionSpec as P

epsilon = 1e-06
INNER_BITS = 3
BUILD_ROWS = 64


def partner(me, mask):
    other = me
    bit = 0
    while mask >> bit:
        if (mask >> bit) & 1:
            size = 1 << bit
            other = other + size * (1 - 2 * lax.rem(lax.div(me, size), 2))
        bit += 1
    return other


def dot(a, b):
    return jnp.dot(a, b, preferred_element_type=jnp.float32)


def dot_rows(a, b):
    return lax.dot_general(a, b, (((0,), (0,)), ((), ())), preferred_element_type=jnp.float32)


def dot_cols(a, b):
    return lax.dot_general(a, b, (((1,), (1,)), ((), ())), preferred_element_type=jnp.float32)


def kernel(
    inner, outer, levels, bnd,
    feat_ref, w_self_ref, w_neigh_ref, slots_ref, degree_ref, boundary_ref, up_ref,
    hidden_ref, node_ref, step_ref,
    table, pick, out_rows, in_rows, out_grads, in_grads,
    stack, part_in, part, plane_in, gathered,
    row_ss, row_rs, grad_ss, grad_rs, part_ss, part_rs, plane_ss, plane_rs, gather_ss, gather_rs,
):
    me = lax.axis_index("dom")
    nodes = feat_ref.shape[0]
    slot_count = slots_ref.shape[0]
    total_rows = table.shape[0]
    chunk = stack.shape[0] // inner
    mine = lax.rem(me, inner)

    inner_masks = list(range(1, inner))
    outer_masks = [e * inner for e in range(1, outer)]
    barrier = pltpu.get_barrier_semaphore()
    for mask in inner_masks + outer_masks:
        pl.semaphore_signal(
            barrier, inc=1, device_id=(partner(me, mask),), device_id_type=pl.DeviceIdType.MESH
        )

    def remote(src, dst, send_sem, recv_sem, mask):
        return pltpu.make_async_remote_copy(
            src_ref=src, dst_ref=dst, send_sem=send_sem, recv_sem=recv_sem,
            device_id=(partner(me, mask),), device_id_type=pl.DeviceIdType.MESH,
        )

    feat = feat_ref[...]

    row_id = lax.broadcasted_iota(jnp.int32, (nodes, bnd), 0)
    row_copies = [None] * levels
    for place, level in enumerate(reversed(range(levels))):
        hot = (row_id == boundary_ref[level]).astype(jnp.float32).astype(jnp.bfloat16)
        span = pl.ds(level * bnd, bnd)
        pick[:, span] = hot
        out_rows[span, :] = dot_rows(hot, feat).astype(jnp.bfloat16)
        if place == 0:
            pl.semaphore_wait(barrier, len(inner_masks) + len(outer_masks))
        row_copies[level] = remote(
            out_rows.at[span, :], in_rows.at[span, :], row_ss.at[level], row_rs.at[level], 1 << level
        )
        row_copies[level].start()

    degree_row = degree_ref[...].reshape(1, nodes)
    named = [
        jnp.where(degree_row > slot, slots_ref[slot : slot + 1, :], -1) for slot in range(slot_count)
    ]

    def build(block, carry):
        start = pl.multiple_of(block * BUILD_ROWS, BUILD_ROWS)
        row = lax.broadcasted_iota(jnp.int32, (BUILD_ROWS, nodes), 0) + start
        count = jnp.zeros((BUILD_ROWS, nodes), jnp.float32)
        for slot in range(slot_count):
            count = jnp.where(row == named[slot], count + 1.0, count)
        table[pl.ds(start, BUILD_ROWS), :] = count.astype(jnp.bfloat16)
        return carry

    lax.fori_loop(0, total_rows // BUILD_ROWS, build, 0)

    share_row = 1.0 / degree_row.astype(jnp.float32)
    share = jnp.transpose(jnp.broadcast_to(share_row, (128, nodes)))
    share = jnp.concatenate([share] * (feat.shape[1] // 128), axis=1)

    summed = dot_rows(table[:nodes, :], feat)
    pre_self = dot(feat, w_self_ref[...])
    for level in range(levels):
        row_copies[level].wait_recv()
    summed = summed + dot_rows(table[nodes:, :], in_rows[...])
    agg = (summed * share).astype(jnp.bfloat16)
    pre_sum = pre_self + dot(agg, w_neigh_ref[...])
    sigmoid = jax.nn.sigmoid(pre_sum)
    hidden_ref[...] = (pre_sum * sigmoid).astype(jnp.bfloat16)
    pre_grad = (
        up_ref[...].astype(jnp.float32) * sigmoid * (1.0 + pre_sum * (1.0 - sigmoid))
    ).astype(jnp.bfloat16)

    width = feat.shape[1]
    stack[:width, :] = dot_rows(feat, pre_grad).astype(jnp.bfloat16)
    stack[width:, :] = dot_rows(agg, pre_grad).astype(jnp.bfloat16)
    part_copies = []
    for mask in inner_masks:
        theirs = lax.rem(partner(me, mask), inner)
        copy = remote(
            stack.at[pl.ds(pl.multiple_of(theirs * chunk, chunk), chunk), :],
            part_in.at[mask], part_ss.at[mask], part_rs.at[mask], mask,
        )
        copy.start()
        part_copies.append(copy)

    slot_share = (dot_cols(pre_grad, w_neigh_ref[...]) * share).astype(jnp.bfloat16)
    out_grads[...] = dot(table[nodes:, :], slot_share).astype(jnp.bfloat16)
    grad_copies = []
    for level in reversed(range(levels)):
        span = pl.ds(level * bnd, bnd)
        copy = remote(
            out_grads.at[span, :], in_grads.at[span, :], grad_ss.at[level], grad_rs.at[level], 1 << level
        )
        copy.start()
        grad_copies.append(copy)
    local = dot_cols(pre_grad, w_self_ref[...]) + dot(table[:nodes, :], slot_share)

    own = pl.ds(pl.multiple_of(mine * chunk, chunk), chunk)
    for copy in part_copies:
        copy.wait_recv()
    total = stack[own, :].astype(jnp.float32)
    for mask in inner_masks:
        total = total + part_in[mask].astype(jnp.float32)
    part[...] = total.astype(jnp.bfloat16)
    plane_copies = []
    for index, mask in enumerate(outer_masks):
        copy = remote(part, plane_in.at[index + 1], plane_ss.at[index + 1], plane_rs.at[index + 1], mask)
        copy.start()
        plane_copies.append(copy)

    for copy in grad_copies:
        copy.wait_recv()
    node_ref[...] = (local + dot(pick[...], in_grads[...])).astype(jnp.bfloat16)

    for copy in plane_copies:
        copy.wait_recv()
    terms = [part[...].astype(jnp.float32)]
    for index in range(1, outer):
        terms.append(plane_in[index].astype(jnp.float32))
    while len(terms) > 1:
        terms = [terms[i] + terms[i + 1] for i in range(0, len(terms), 2)]
    gathered[own, :] = terms[0].astype(jnp.bfloat16)
    gather_copies = []
    for mask in inner_masks:
        copy = remote(
            gathered.at[own, :], gathered.at[own, :], gather_ss.at[mask], gather_rs.at[mask], mask
        )
        copy.start()
        gather_copies.append(copy)
    for copy in gather_copies:
        copy.wait_recv()
    whole = gathered[...].astype(jnp.float32)
    step_ref[...] = whole * lax.rsqrt(jnp.mean(whole * whole) + epsilon)

    for copy in row_copies + part_copies + grad_copies + plane_copies + gather_copies:
        copy.wait_send()


def per_device(features, w_self, w_neigh, neighbors, degree, boundary, upstream):
    size = lax.axis_size("dom")
    levels = size.bit_length() - 1
    inner = min(size, 1 << INNER_BITS)
    outer = size // inner
    nodes, width = features.shape
    bnd = boundary.shape[2]
    rows = levels * bnd
    chunk = 2 * width // inner
    bf16 = jnp.bfloat16
    sem = pltpu.SemaphoreType.DMA
    vmem = pl.BlockSpec(memory_space=pltpu.VMEM)
    return pl.pallas_call(
        functools.partial(kernel, inner, outer, levels, bnd),
        out_shape=(
            jax.ShapeDtypeStruct((nodes, width), bf16),
            jax.ShapeDtypeStruct((nodes, width), bf16),
            jax.ShapeDtypeStruct((2 * width, width), jnp.float32),
        ),
        in_specs=[vmem] * 7,
        out_specs=(vmem, vmem, vmem),
        scratch_shapes=[
            pltpu.VMEM((nodes + rows, nodes), bf16),
            pltpu.VMEM((nodes, rows), bf16),
            pltpu.VMEM((rows, width), bf16),
            pltpu.VMEM((rows, width), bf16),
            pltpu.VMEM((rows, width), bf16),
            pltpu.VMEM((rows, width), bf16),
            pltpu.VMEM((2 * width, width), bf16),
            pltpu.VMEM((inner, chunk, width), bf16),
            pltpu.VMEM((chunk, width), bf16),
            pltpu.VMEM((outer, chunk, width), bf16),
            pltpu.VMEM((2 * width, width), bf16),
            sem((levels,)), sem((levels,)), sem((levels,)), sem((levels,)),
            sem((inner,)), sem((inner,)), sem((outer,)), sem((outer,)), sem((inner,)), sem((inner,)),
        ],
        compiler_params=pltpu.CompilerParams(
            collective_id=0, has_side_effects=True, vmem_limit_bytes=40 << 20
        ),
        cost_estimate=pl.CostEstimate(flops=1 << 30, bytes_accessed=3 << 20, transcendentals=nodes * width),
    )(features, w_self, w_neigh, neighbors.T, degree, boundary.transpose(1, 0, 2), upstream)


def solution(mesh):
    return jax.shard_map(
        per_device,
        mesh=mesh,
        in_specs=(
            P("dom", None),
            P(),
            P(),
            P("dom", None),
            P("dom"),
            P("dom", None, None),
            P("dom", None),
        ),
        out_specs=(P("dom", None), P("dom", None), P()),
        check_vma=False,
    )
```

```python
import functools

import jax
import jax.numpy as jnp
from jax import lax
from jax.experimental import pallas as pl
from jax.experimental.pallas import tpu as pltpu
from jax.sharding import PartitionSpec as P

epsilon = 1e-06
INNER_BITS = 3
BUILD_ROWS = 64


def partner(me, mask):
    other = me
    bit = 0
    while mask >> bit:
        if (mask >> bit) & 1:
            size = 1 << bit
            other = other + size * (1 - 2 * lax.rem(lax.div(me, size), 2))
        bit += 1
    return other


def dot(a, b):
    return jnp.dot(a, b, preferred_element_type=jnp.float32)


def dot_rows(a, b):
    return lax.dot_general(a, b, (((0,), (0,)), ((), ())), preferred_element_type=jnp.float32)


def dot_cols(a, b):
    return lax.dot_general(a, b, (((1,), (1,)), ((), ())), preferred_element_type=jnp.float32)


def kernel(
    inner, outer, levels, bnd,
    feat_hbm, w_self_hbm, w_neigh_hbm, slots_hbm, degree_hbm, boundary_hbm, up_hbm,
    hidden_ref, node_ref, gathered,
    feat_ref, w_self_ref, w_neigh_ref, slots_ref, degree_ref, boundary_ref, up_ref, fetch_sem,
    table, pick, out_rows, in_rows, out_grads, in_grads,
    stack, part_in, part, plane_in,
    row_ss, row_rs, grad_ss, grad_rs, part_ss, part_rs, plane_ss, plane_rs, gather_ss, gather_rs,
):
    me = lax.axis_index("dom")
    nodes = feat_ref.shape[0]
    slot_count = slots_ref.shape[0]
    total_rows = table.shape[0]
    chunk = stack.shape[0] // inner
    mine = lax.rem(me, inner)

    fetches = [
        pltpu.make_async_copy(src, dst, fetch_sem.at[index])
        for index, (src, dst) in enumerate((
            (boundary_hbm, boundary_ref), (feat_hbm, feat_ref), (degree_hbm, degree_ref),
            (slots_hbm, slots_ref), (w_self_hbm, w_self_ref), (w_neigh_hbm, w_neigh_ref),
            (up_hbm, up_ref),
        ))
    ]
    for fetch in fetches:
        fetch.start()

    inner_masks = list(range(1, inner))
    outer_masks = [e * inner for e in range(1, outer)]
    barrier = pltpu.get_barrier_semaphore()
    for mask in inner_masks + outer_masks:
        pl.semaphore_signal(
            barrier, inc=1, device_id=(partner(me, mask),), device_id_type=pl.DeviceIdType.MESH
        )

    def remote(src, dst, send_sem, recv_sem, mask):
        return pltpu.make_async_remote_copy(
            src_ref=src, dst_ref=dst, send_sem=send_sem, recv_sem=recv_sem,
            device_id=(partner(me, mask),), device_id_type=pl.DeviceIdType.MESH,
        )

    fetches[0].wait()
    fetches[1].wait()
    feat = feat_ref[...]

    row_id = lax.broadcasted_iota(jnp.int32, (nodes, bnd), 0)
    row_copies = [None] * levels
    for place, level in enumerate(reversed(range(levels))):
        hot = (row_id == boundary_ref[level]).astype(jnp.float32).astype(jnp.bfloat16)
        span = pl.ds(level * bnd, bnd)
        pick[:, span] = hot
        out_rows[span, :] = dot_rows(hot, feat).astype(jnp.bfloat16)
        if place == 0:
            pl.semaphore_wait(barrier, len(inner_masks) + len(outer_masks))
        row_copies[level] = remote(
            out_rows.at[span, :], in_rows.at[span, :], row_ss.at[level], row_rs.at[level], 1 << level
        )
        row_copies[level].start()

    fetches[2].wait()
    fetches[3].wait()
    degree_row = degree_ref[...].reshape(1, nodes)
    named = [
        jnp.where(degree_row > slot, slots_ref[slot : slot + 1, :], -1) for slot in range(slot_count)
    ]

    def build(block, carry):
        start = pl.multiple_of(block * BUILD_ROWS, BUILD_ROWS)
        row = lax.broadcasted_iota(jnp.int32, (BUILD_ROWS, nodes), 0) + start
        count = jnp.zeros((BUILD_ROWS, nodes), jnp.float32)
        for slot in range(slot_count):
            count = jnp.where(row == named[slot], count + 1.0, count)
        table[pl.ds(start, BUILD_ROWS), :] = count.astype(jnp.bfloat16)
        return carry

    lax.fori_loop(0, total_rows // BUILD_ROWS, build, 0)

    share_row = 1.0 / degree_row.astype(jnp.float32)
    share = jnp.transpose(jnp.broadcast_to(share_row, (128, nodes)))
    share = jnp.concatenate([share] * (feat.shape[1] // 128), axis=1)

    summed = dot_rows(table[:nodes, :], feat)
    for fetch in fetches[4:]:
        fetch.wait()
    pre_self = dot(feat, w_self_ref[...])
    for level in range(levels):
        row_copies[level].wait_recv()
    summed = summed + dot_rows(table[nodes:, :], in_rows[...])
    agg = (summed * share).astype(jnp.bfloat16)
    pre_sum = pre_self + dot(agg, w_neigh_ref[...])
    sigmoid = jax.nn.sigmoid(pre_sum)
    hidden_ref[...] = (pre_sum * sigmoid).astype(jnp.bfloat16)
    pre_grad = (
        up_ref[...].astype(jnp.float32) * sigmoid * (1.0 + pre_sum * (1.0 - sigmoid))
    ).astype(jnp.bfloat16)

    width = feat.shape[1]
    stack[:width, :] = dot_rows(feat, pre_grad).astype(jnp.bfloat16)
    stack[width:, :] = dot_rows(agg, pre_grad).astype(jnp.bfloat16)
    part_copies = []
    for mask in inner_masks:
        theirs = lax.rem(partner(me, mask), inner)
        copy = remote(
            stack.at[pl.ds(pl.multiple_of(theirs * chunk, chunk), chunk), :],
            part_in.at[mask], part_ss.at[mask], part_rs.at[mask], mask,
        )
        copy.start()
        part_copies.append(copy)

    slot_share = (dot_cols(pre_grad, w_neigh_ref[...]) * share).astype(jnp.bfloat16)
    out_grads[...] = dot(table[nodes:, :], slot_share).astype(jnp.bfloat16)
    grad_copies = []
    for level in reversed(range(levels)):
        span = pl.ds(level * bnd, bnd)
        copy = remote(
            out_grads.at[span, :], in_grads.at[span, :], grad_ss.at[level], grad_rs.at[level], 1 << level
        )
        copy.start()
        grad_copies.append(copy)
    local = dot_cols(pre_grad, w_self_ref[...]) + dot(table[:nodes, :], slot_share)

    own = pl.ds(pl.multiple_of(mine * chunk, chunk), chunk)
    for copy in part_copies:
        copy.wait_recv()
    total = stack[own, :].astype(jnp.float32)
    for mask in inner_masks:
        total = total + part_in[mask].astype(jnp.float32)
    part[...] = total.astype(jnp.bfloat16)
    plane_copies = []
    for index, mask in enumerate(outer_masks):
        copy = remote(part, plane_in.at[index + 1], plane_ss.at[index + 1], plane_rs.at[index + 1], mask)
        copy.start()
        plane_copies.append(copy)

    for copy in grad_copies:
        copy.wait_recv()
    node_ref[...] = (local + dot(pick[...], in_grads[...])).astype(jnp.bfloat16)

    for copy in plane_copies:
        copy.wait_recv()
    terms = [part[...].astype(jnp.float32)]
    for index in range(1, outer):
        terms.append(plane_in[index].astype(jnp.float32))
    while len(terms) > 1:
        terms = [terms[i] + terms[i + 1] for i in range(0, len(terms), 2)]
    gathered[own, :] = terms[0].astype(jnp.bfloat16)
    gather_copies = []
    for mask in inner_masks:
        copy = remote(
            gathered.at[own, :], gathered.at[own, :], gather_ss.at[mask], gather_rs.at[mask], mask
        )
        copy.start()
        gather_copies.append(copy)
    for copy in gather_copies:
        copy.wait_recv()
    for copy in row_copies + part_copies + grad_copies + plane_copies + gather_copies:
        copy.wait_send()


def finish(hidden, node, gathered, hidden_hbm, node_hbm, step_hbm, step, sems):
    copies = [
        pltpu.make_async_copy(hidden, hidden_hbm, sems.at[0]),
        pltpu.make_async_copy(node, node_hbm, sems.at[1]),
        pltpu.make_async_copy(step, step_hbm, sems.at[2]),
    ]
    copies[0].start()
    copies[1].start()
    whole = gathered[...].astype(jnp.float32)
    step[...] = whole * lax.rsqrt(jnp.mean(whole * whole) + epsilon)
    copies[2].start()
    for copy in copies:
        copy.wait()


def per_device(features, w_self, w_neigh, neighbors, degree, boundary, upstream):
    size = lax.axis_size("dom")
    levels = size.bit_length() - 1
    inner = min(size, 1 << INNER_BITS)
    outer = size // inner
    nodes, width = features.shape
    bnd = boundary.shape[2]
    rows = levels * bnd
    chunk = 2 * width // inner
    bf16 = jnp.bfloat16
    sem = pltpu.SemaphoreType.DMA
    vmem = pl.BlockSpec(memory_space=pltpu.VMEM)
    hbm = pl.BlockSpec(memory_space=pltpu.HBM)
    args = (features, w_self, w_neigh, neighbors.T, degree, boundary.transpose(1, 0, 2), upstream)
    args = tuple(pltpu.with_memory_space_constraint(arg, pltpu.HBM) for arg in args)
    hidden, node, gathered = pl.pallas_call(
        functools.partial(kernel, inner, outer, levels, bnd),
        out_shape=(
            pltpu.VMEM((nodes, width), bf16),
            pltpu.VMEM((nodes, width), bf16),
            pltpu.VMEM((2 * width, width), bf16),
        ),
        in_specs=[hbm] * 7,
        out_specs=(vmem, vmem, vmem),
        scratch_shapes=[pltpu.VMEM(arg.shape, arg.dtype) for arg in args] + [
            sem((7,)),
            pltpu.VMEM((nodes + rows, nodes), bf16),
            pltpu.VMEM((nodes, rows), bf16),
            pltpu.VMEM((rows, width), bf16),
            pltpu.VMEM((rows, width), bf16),
            pltpu.VMEM((rows, width), bf16),
            pltpu.VMEM((rows, width), bf16),
            pltpu.VMEM((2 * width, width), bf16),
            pltpu.VMEM((inner, chunk, width), bf16),
            pltpu.VMEM((chunk, width), bf16),
            pltpu.VMEM((outer, chunk, width), bf16),
            sem((levels,)), sem((levels,)), sem((levels,)), sem((levels,)),
            sem((inner,)), sem((inner,)), sem((outer,)), sem((outer,)), sem((inner,)), sem((inner,)),
        ],
        compiler_params=pltpu.CompilerParams(
            collective_id=0, has_side_effects=True, vmem_limit_bytes=40 << 20
        ),
        cost_estimate=pl.CostEstimate(flops=1 << 30, bytes_accessed=3 << 20, transcendentals=nodes * width),
    )(*args)
    return pl.pallas_call(
        finish,
        out_shape=(
            jax.ShapeDtypeStruct((nodes, width), bf16),
            jax.ShapeDtypeStruct((nodes, width), bf16),
            jax.ShapeDtypeStruct((2 * width, width), jnp.float32),
        ),
        in_specs=[vmem] * 3,
        out_specs=(hbm, hbm, hbm),
        scratch_shapes=[pltpu.VMEM((2 * width, width), jnp.float32), sem((3,))],
        compiler_params=pltpu.CompilerParams(vmem_limit_bytes=16 << 20),
        cost_estimate=pl.CostEstimate(flops=1 << 18, bytes_accessed=1 << 20, transcendentals=0),
    )(hidden, node, gathered)


def solution(mesh):
    return jax.shard_map(
        per_device,
        mesh=mesh,
        in_specs=(
            P("dom", None),
            P(),
            P(),
            P("dom", None),
            P("dom"),
            P("dom", None, None),
            P("dom", None),
        ),
        out_specs=(P("dom", None), P("dom", None), P()),
        check_vma=False,
    )
```

```python
import functools

import jax
import jax.numpy as jnp
from jax import lax
from jax.experimental import pallas as pl
from jax.experimental.pallas import tpu as pltpu
from jax.sharding import PartitionSpec as P

epsilon = 1e-06
INNER_BITS = 3
BUILD_ROWS = 64


def partner(me, mask):
    other = me
    bit = 0
    while mask >> bit:
        if (mask >> bit) & 1:
            size = 1 << bit
            other = other + size * (1 - 2 * lax.rem(lax.div(me, size), 2))
        bit += 1
    return other


def dot(a, b):
    return jnp.dot(a, b, preferred_element_type=jnp.float32)


def dot_rows(a, b):
    return lax.dot_general(a, b, (((0,), (0,)), ((), ())), preferred_element_type=jnp.float32)


def dot_cols(a, b):
    return lax.dot_general(a, b, (((1,), (1,)), ((), ())), preferred_element_type=jnp.float32)


def kernel(
    inner, outer, levels, bnd,
    feat_hbm, w_self_hbm, w_neigh_hbm, slots_hbm, degree_hbm, boundary_hbm, up_hbm,
    hidden_ref, node_ref, gathered,
    feat_ref, w_self_ref, w_neigh_ref, slots_ref, degree_ref, boundary_ref, up_ref, fetch_sem,
    table, pick, out_rows, in_rows, out_grads, in_grads,
    stack, part_in, part, plane_in,
    row_ss, row_rs, grad_ss, grad_rs, part_ss, part_rs, plane_ss, plane_rs, gather_ss, gather_rs,
):
    me = lax.axis_index("dom")
    nodes = feat_ref.shape[0]
    slot_count = slots_ref.shape[0]
    total_rows = table.shape[0]
    chunk = stack.shape[1] // inner
    mine = lax.rem(me, inner)

    fetches = [
        pltpu.make_async_copy(src, dst, fetch_sem.at[index])
        for index, (src, dst) in enumerate((
            (boundary_hbm, boundary_ref), (feat_hbm, feat_ref), (degree_hbm, degree_ref),
            (slots_hbm, slots_ref), (w_self_hbm, w_self_ref), (w_neigh_hbm, w_neigh_ref),
            (up_hbm, up_ref),
        ))
    ]
    for fetch in fetches:
        fetch.start()

    inner_masks = list(range(1, inner))
    outer_masks = [e * inner for e in range(1, outer)]
    barrier = pltpu.get_barrier_semaphore()
    for mask in inner_masks + outer_masks:
        pl.semaphore_signal(
            barrier, inc=1, device_id=(partner(me, mask),), device_id_type=pl.DeviceIdType.MESH
        )

    def remote(src, dst, send_sem, recv_sem, mask):
        return pltpu.make_async_remote_copy(
            src_ref=src, dst_ref=dst, send_sem=send_sem, recv_sem=recv_sem,
            device_id=(partner(me, mask),), device_id_type=pl.DeviceIdType.MESH,
        )

    fetches[0].wait()
    fetches[1].wait()
    feat = feat_ref[...]

    row_id = lax.broadcasted_iota(jnp.int32, (nodes, bnd), 0)
    row_copies = [None] * levels
    for place, level in enumerate(reversed(range(levels))):
        hot = (row_id == boundary_ref[level]).astype(jnp.float32).astype(jnp.bfloat16)
        span = pl.ds(level * bnd, bnd)
        pick[:, span] = hot
        out_rows[span, :] = dot_rows(hot, feat).astype(jnp.bfloat16)
        if place == 0:
            pl.semaphore_wait(barrier, len(inner_masks) + len(outer_masks))
        row_copies[level] = remote(
            out_rows.at[span, :], in_rows.at[span, :], row_ss.at[level], row_rs.at[level], 1 << level
        )
        row_copies[level].start()

    fetches[2].wait()
    fetches[3].wait()
    degree_row = degree_ref[...].reshape(1, nodes)
    named = [
        jnp.where(degree_row > slot, slots_ref[slot : slot + 1, :], -1) for slot in range(slot_count)
    ]

    def build(block, carry):
        start = pl.multiple_of(block * BUILD_ROWS, BUILD_ROWS)
        row = lax.broadcasted_iota(jnp.int32, (BUILD_ROWS, nodes), 0) + start
        count = jnp.zeros((BUILD_ROWS, nodes), jnp.float32)
        for slot in range(slot_count):
            count = jnp.where(row == named[slot], count + 1.0, count)
        table[pl.ds(start, BUILD_ROWS), :] = count.astype(jnp.bfloat16)
        return carry

    lax.fori_loop(0, total_rows // BUILD_ROWS, build, 0)

    share_row = 1.0 / degree_row.astype(jnp.float32)
    share = jnp.transpose(jnp.broadcast_to(share_row, (128, nodes)))
    share = jnp.concatenate([share] * (feat.shape[1] // 128), axis=1)

    summed = dot_rows(table[:nodes, :], feat)
    for fetch in fetches[4:]:
        fetch.wait()
    pre_self = dot(feat, w_self_ref[...])
    for level in range(levels):
        row_copies[level].wait_recv()
    summed = summed + dot_rows(table[nodes:, :], in_rows[...])
    agg = (summed * share).astype(jnp.bfloat16)
    pre_sum = pre_self + dot(agg, w_neigh_ref[...])
    sigmoid = jax.nn.sigmoid(pre_sum)
    hidden_ref[...] = (pre_sum * sigmoid).astype(jnp.bfloat16)
    pre_grad = (
        up_ref[...].astype(jnp.float32) * sigmoid * (1.0 + pre_sum * (1.0 - sigmoid))
    ).astype(jnp.bfloat16)

    width = feat.shape[1]
    part_copies = []
    for half, left in enumerate((feat, agg)):
        stack[half] = dot_rows(left, pre_grad).astype(jnp.bfloat16)
        for mask in inner_masks:
            theirs = lax.rem(partner(me, mask), inner)
            copy = remote(
                stack.at[half, pl.ds(pl.multiple_of(theirs * chunk, chunk), chunk), :],
                part_in.at[half, mask], part_ss.at[half, mask], part_rs.at[half, mask], mask,
            )
            copy.start()
            part_copies.append(copy)

    slot_share = (dot_cols(pre_grad, w_neigh_ref[...]) * share).astype(jnp.bfloat16)
    out_grads[...] = dot(table[nodes:, :], slot_share).astype(jnp.bfloat16)
    grad_copies = []

    def return_grads(level):
        span = pl.ds(level * bnd, bnd)
        copy = remote(
            out_grads.at[span, :], in_grads.at[span, :], grad_ss.at[level], grad_rs.at[level], 1 << level
        )
        copy.start()
        grad_copies.append(copy)

    inner_levels = inner.bit_length() - 1
    for level in range(inner_levels):
        return_grads(level)
    local = dot_cols(pre_grad, w_self_ref[...]) + dot(table[:nodes, :], slot_share)

    own = pl.ds(pl.multiple_of(mine * chunk, chunk), chunk)
    per_half = len(inner_masks)
    plane_copies = []
    for half in range(2):
        for copy in part_copies[half * per_half : (half + 1) * per_half]:
            copy.wait_recv()
        total = stack[half, own, :].astype(jnp.float32)
        for mask in inner_masks:
            total = total + part_in[half, mask].astype(jnp.float32)
        part[half] = total.astype(jnp.bfloat16)
        for index, mask in enumerate(outer_masks):
            copy = remote(
                part.at[half], plane_in.at[half, index + 1],
                plane_ss.at[half, index + 1], plane_rs.at[half, index + 1], mask,
            )
            copy.start()
            plane_copies.append(copy)
    for level in range(inner_levels, levels):
        return_grads(level)

    per_outer = len(outer_masks)
    gather_copies = []
    for half in range(2):
        for copy in plane_copies[half * per_outer : (half + 1) * per_outer]:
            copy.wait_recv()
        terms = [part[half].astype(jnp.float32)]
        for index in range(1, outer):
            terms.append(plane_in[half, index].astype(jnp.float32))
        while len(terms) > 1:
            terms = [terms[i] + terms[i + 1] for i in range(0, len(terms), 2)]
        rows = pl.ds(pl.multiple_of(half * width + mine * chunk, chunk), chunk)
        gathered[rows, :] = terms[0].astype(jnp.bfloat16)
        for mask in inner_masks:
            copy = remote(
                gathered.at[rows, :], gathered.at[rows, :],
                gather_ss.at[half, mask], gather_rs.at[half, mask], mask,
            )
            copy.start()
            gather_copies.append(copy)

    for copy in grad_copies:
        copy.wait_recv()
    node_ref[...] = (local + dot(pick[...], in_grads[...])).astype(jnp.bfloat16)
    for copy in gather_copies:
        copy.wait_recv()

    for copy in row_copies + part_copies + grad_copies + plane_copies + gather_copies:
        copy.wait_send()


def finish(hidden, node, gathered, hidden_hbm, node_hbm, step_hbm, step, sems):
    copies = [
        pltpu.make_async_copy(hidden, hidden_hbm, sems.at[0]),
        pltpu.make_async_copy(node, node_hbm, sems.at[1]),
        pltpu.make_async_copy(step, step_hbm, sems.at[2]),
    ]
    copies[0].start()
    copies[1].start()
    whole = gathered[...].astype(jnp.float32)
    step[...] = whole * lax.rsqrt(jnp.mean(whole * whole) + epsilon)
    copies[2].start()
    for copy in copies:
        copy.wait()


def per_device(features, w_self, w_neigh, neighbors, degree, boundary, upstream):
    size = lax.axis_size("dom")
    levels = size.bit_length() - 1
    inner = min(size, 1 << INNER_BITS)
    outer = size // inner
    nodes, width = features.shape
    bnd = boundary.shape[2]
    rows = levels * bnd
    chunk = width // inner
    bf16 = jnp.bfloat16
    sem = pltpu.SemaphoreType.DMA
    vmem = pl.BlockSpec(memory_space=pltpu.VMEM)
    hbm = pl.BlockSpec(memory_space=pltpu.HBM)
    args = (features, w_self, w_neigh, neighbors.T, degree, boundary.transpose(1, 0, 2), upstream)
    args = tuple(pltpu.with_memory_space_constraint(arg, pltpu.HBM) for arg in args)
    hidden, node, gathered = pl.pallas_call(
        functools.partial(kernel, inner, outer, levels, bnd),
        out_shape=(
            pltpu.VMEM((nodes, width), bf16),
            pltpu.VMEM((nodes, width), bf16),
            pltpu.VMEM((2 * width, width), bf16),
        ),
        in_specs=[hbm] * 7,
        out_specs=(vmem, vmem, vmem),
        scratch_shapes=[pltpu.VMEM(arg.shape, arg.dtype) for arg in args] + [
            sem((7,)),
            pltpu.VMEM((nodes + rows, nodes), bf16),
            pltpu.VMEM((nodes, rows), bf16),
            pltpu.VMEM((rows, width), bf16),
            pltpu.VMEM((rows, width), bf16),
            pltpu.VMEM((rows, width), bf16),
            pltpu.VMEM((rows, width), bf16),
            pltpu.VMEM((2, width, width), bf16),
            pltpu.VMEM((2, inner, chunk, width), bf16),
            pltpu.VMEM((2, chunk, width), bf16),
            pltpu.VMEM((2, outer, chunk, width), bf16),
            sem((levels,)), sem((levels,)), sem((levels,)), sem((levels,)),
            sem((2, inner)), sem((2, inner)), sem((2, outer)), sem((2, outer)), sem((2, inner)), sem((2, inner)),
        ],
        compiler_params=pltpu.CompilerParams(
            collective_id=0, has_side_effects=True, vmem_limit_bytes=40 << 20
        ),
        cost_estimate=pl.CostEstimate(flops=1 << 30, bytes_accessed=3 << 20, transcendentals=nodes * width),
    )(*args)
    return pl.pallas_call(
        finish,
        out_shape=(
            jax.ShapeDtypeStruct((nodes, width), bf16),
            jax.ShapeDtypeStruct((nodes, width), bf16),
            jax.ShapeDtypeStruct((2 * width, width), jnp.float32),
        ),
        in_specs=[vmem] * 3,
        out_specs=(hbm, hbm, hbm),
        scratch_shapes=[pltpu.VMEM((2 * width, width), jnp.float32), sem((3,))],
        compiler_params=pltpu.CompilerParams(vmem_limit_bytes=16 << 20),
        cost_estimate=pl.CostEstimate(flops=1 << 18, bytes_accessed=1 << 20, transcendentals=0),
    )(hidden, node, gathered)


def solution(mesh):
    return jax.shard_map(
        per_device,
        mesh=mesh,
        in_specs=(
            P("dom", None),
            P(),
            P(),
            P("dom", None),
            P("dom"),
            P("dom", None, None),
            P("dom", None),
        ),
        out_specs=(P("dom", None), P("dom", None), P()),
        check_vma=False,
    )
```

```python
import functools

import jax
import jax.numpy as jnp
from jax import lax
from jax.experimental import pallas as pl
from jax.experimental.pallas import tpu as pltpu
from jax.sharding import PartitionSpec as P

epsilon = 1e-06
INNER_BITS = 3
BUILD_ROWS = 128


def partner(me, mask):
    other = me
    bit = 0
    while mask >> bit:
        if (mask >> bit) & 1:
            size = 1 << bit
            other = other + size * (1 - 2 * lax.rem(lax.div(me, size), 2))
        bit += 1
    return other


def dot(a, b):
    return jnp.dot(a, b, preferred_element_type=jnp.float32)


def dot_rows(a, b):
    return lax.dot_general(a, b, (((0,), (0,)), ((), ())), preferred_element_type=jnp.float32)


def dot_cols(a, b):
    return lax.dot_general(a, b, (((1,), (1,)), ((), ())), preferred_element_type=jnp.float32)


def kernel(
    inner, outer, levels, bnd,
    feat_hbm, w_self_hbm, w_neigh_hbm, slots_hbm, degree_hbm, boundary_hbm, up_hbm,
    hidden_ref, node_ref, gathered,
    feat_ref, w_self_ref, w_neigh_ref, slots_ref, degree_ref, boundary_ref, up_ref, fetch_sem,
    table, table_t, pick, out_rows, in_rows, out_grads, in_grads,
    stack, part_in, part, plane_in,
    row_ss, row_rs, grad_ss, grad_rs, part_ss, part_rs, plane_ss, plane_rs, gather_ss, gather_rs,
):
    me = lax.axis_index("dom")
    nodes = feat_ref.shape[0]
    slot_count = slots_ref.shape[0]
    total_rows = table.shape[0]
    chunk = stack.shape[1] // inner
    mine = lax.rem(me, inner)

    fetches = [
        pltpu.make_async_copy(src, dst, fetch_sem.at[index])
        for index, (src, dst) in enumerate((
            (boundary_hbm, boundary_ref), (feat_hbm, feat_ref), (degree_hbm, degree_ref),
            (slots_hbm, slots_ref), (w_self_hbm, w_self_ref), (w_neigh_hbm, w_neigh_ref),
            (up_hbm, up_ref),
        ))
    ]
    for fetch in fetches:
        fetch.start()

    inner_masks = list(range(1, inner))
    outer_masks = [e * inner for e in range(1, outer)]
    barrier = pltpu.get_barrier_semaphore()
    for mask in inner_masks + outer_masks:
        pl.semaphore_signal(
            barrier, inc=1, device_id=(partner(me, mask),), device_id_type=pl.DeviceIdType.MESH
        )

    def remote(src, dst, send_sem, recv_sem, mask):
        return pltpu.make_async_remote_copy(
            src_ref=src, dst_ref=dst, send_sem=send_sem, recv_sem=recv_sem,
            device_id=(partner(me, mask),), device_id_type=pl.DeviceIdType.MESH,
        )

    fetches[0].wait()
    fetches[1].wait()
    feat = feat_ref[...]

    row_id = lax.broadcasted_iota(jnp.int32, (nodes, bnd), 0)
    row_copies = [None] * levels
    for place, level in enumerate(reversed(range(levels))):
        hot = (row_id == boundary_ref[level]).astype(jnp.float32).astype(jnp.bfloat16)
        span = pl.ds(level * bnd, bnd)
        pick[:, span] = hot
        out_rows[span, :] = dot_rows(hot, feat).astype(jnp.bfloat16)
        if place == 0:
            pl.semaphore_wait(barrier, len(inner_masks) + len(outer_masks))
        row_copies[level] = remote(
            out_rows.at[span, :], in_rows.at[span, :], row_ss.at[level], row_rs.at[level], 1 << level
        )
        row_copies[level].start()

    fetches[2].wait()
    fetches[3].wait()
    degree_row = degree_ref[...].reshape(1, nodes)
    named = [
        jnp.where(degree_row > slot, slots_ref[slot : slot + 1, :], -1) for slot in range(slot_count)
    ]

    named = jnp.concatenate(named, axis=0).astype(jnp.float32)
    row = lax.broadcasted_iota(jnp.int32, (BUILD_ROWS, nodes), 0).astype(jnp.float32).astype(jnp.bfloat16)

    def build(block, carry):
        start = pl.multiple_of(block * BUILD_ROWS, BUILD_ROWS)
        shifted = (named - start.astype(jnp.float32)).astype(jnp.bfloat16)
        count = jnp.zeros((BUILD_ROWS, nodes), jnp.bfloat16)
        for slot in range(slot_count):
            count = jnp.where(row == shifted[slot : slot + 1, :], count + 1, count)
        table[pl.ds(start, BUILD_ROWS), :] = count
        return carry

    lax.fori_loop(0, total_rows // BUILD_ROWS, build, 0)

    share_row = 1.0 / degree_row.astype(jnp.float32)
    share = jnp.transpose(jnp.broadcast_to(share_row, (128, nodes)))
    share = jnp.concatenate([share] * (feat.shape[1] // 128), axis=1)

    table_t[...] = jnp.transpose(table[nodes:, :])
    feat_t = jnp.transpose(feat)
    summed = dot_rows(table[:nodes, :], feat)
    for fetch in fetches[4:]:
        fetch.wait()
    pre_self = dot(feat, w_self_ref[...])
    inner_levels = inner.bit_length() - 1
    near = inner_levels * bnd
    for level in range(inner_levels):
        row_copies[level].wait_recv()
    summed = summed + dot(table_t[:, :near], in_rows[:near, :])
    for level in range(inner_levels, levels):
        row_copies[level].wait_recv()
    summed = summed + dot(table_t[:, near:], in_rows[near:, :])
    agg = (summed * share).astype(jnp.bfloat16)
    pre_sum = pre_self + dot(agg, w_neigh_ref[...])
    sigmoid = jax.nn.sigmoid(pre_sum)
    hidden_ref[...] = (pre_sum * sigmoid).astype(jnp.bfloat16)
    pre_grad = (
        up_ref[...].astype(jnp.float32) * sigmoid * (1.0 + pre_sum * (1.0 - sigmoid))
    ).astype(jnp.bfloat16)

    width = feat.shape[1]
    part_copies = []
    for half in range(2):
        left_t = feat_t if half == 0 else jnp.transpose(agg)
        stack[half] = dot(left_t, pre_grad).astype(jnp.bfloat16)
        for mask in inner_masks:
            theirs = lax.rem(partner(me, mask), inner)
            copy = remote(
                stack.at[half, pl.ds(pl.multiple_of(theirs * chunk, chunk), chunk), :],
                part_in.at[half, mask], part_ss.at[half, mask], part_rs.at[half, mask], mask,
            )
            copy.start()
            part_copies.append(copy)

    slot_share = (dot_cols(pre_grad, w_neigh_ref[...]) * share).astype(jnp.bfloat16)
    out_grads[...] = dot(table[nodes:, :], slot_share).astype(jnp.bfloat16)
    grad_copies = []

    def return_grads(level):
        span = pl.ds(level * bnd, bnd)
        copy = remote(
            out_grads.at[span, :], in_grads.at[span, :], grad_ss.at[level], grad_rs.at[level], 1 << level
        )
        copy.start()
        grad_copies.append(copy)

    for level in range(inner_levels):
        return_grads(level)
    local = dot_cols(pre_grad, w_self_ref[...]) + dot(table[:nodes, :], slot_share)

    own = pl.ds(pl.multiple_of(mine * chunk, chunk), chunk)
    per_half = len(inner_masks)
    plane_copies = []
    for half in range(2):
        for copy in part_copies[half * per_half : (half + 1) * per_half]:
            copy.wait_recv()
        total = stack[half, own, :].astype(jnp.float32)
        for mask in inner_masks:
            total = total + part_in[half, mask].astype(jnp.float32)
        part[half] = total.astype(jnp.bfloat16)
        for index, mask in enumerate(outer_masks):
            copy = remote(
                part.at[half], plane_in.at[half, index + 1],
                plane_ss.at[half, index + 1], plane_rs.at[half, index + 1], mask,
            )
            copy.start()
            plane_copies.append(copy)
    for level in range(inner_levels, levels):
        return_grads(level)

    per_outer = len(outer_masks)
    gather_copies = []
    for half in range(2):
        for copy in plane_copies[half * per_outer : (half + 1) * per_outer]:
            copy.wait_recv()
        terms = [part[half].astype(jnp.float32)]
        for index in range(1, outer):
            terms.append(plane_in[half, index].astype(jnp.float32))
        while len(terms) > 1:
            terms = [terms[i] + terms[i + 1] for i in range(0, len(terms), 2)]
        rows = pl.ds(pl.multiple_of(half * width + mine * chunk, chunk), chunk)
        gathered[rows, :] = terms[0].astype(jnp.bfloat16)
        for mask in inner_masks:
            copy = remote(
                gathered.at[rows, :], gathered.at[rows, :],
                gather_ss.at[half, mask], gather_rs.at[half, mask], mask,
            )
            copy.start()
            gather_copies.append(copy)

    for copy in grad_copies:
        copy.wait_recv()
    node_ref[...] = (local + dot(pick[...], in_grads[...])).astype(jnp.bfloat16)
    for copy in gather_copies:
        copy.wait_recv()

    for copy in row_copies + part_copies + grad_copies + plane_copies + gather_copies:
        copy.wait_send()


def finish(hidden, node, gathered, hidden_hbm, node_hbm, step_hbm, step, sems):
    copies = [
        pltpu.make_async_copy(hidden, hidden_hbm, sems.at[0]),
        pltpu.make_async_copy(node, node_hbm, sems.at[1]),
        pltpu.make_async_copy(step, step_hbm, sems.at[2]),
    ]
    copies[0].start()
    copies[1].start()
    whole = gathered[...].astype(jnp.float32)
    step[...] = whole * lax.rsqrt(jnp.mean(whole * whole) + epsilon)
    copies[2].start()
    for copy in copies:
        copy.wait()


def per_device(features, w_self, w_neigh, neighbors, degree, boundary, upstream):
    size = lax.axis_size("dom")
    levels = size.bit_length() - 1
    inner = min(size, 1 << INNER_BITS)
    outer = size // inner
    nodes, width = features.shape
    bnd = boundary.shape[2]
    rows = levels * bnd
    chunk = width // inner
    bf16 = jnp.bfloat16
    sem = pltpu.SemaphoreType.DMA
    vmem = pl.BlockSpec(memory_space=pltpu.VMEM)
    hbm = pl.BlockSpec(memory_space=pltpu.HBM)
    args = (features, w_self, w_neigh, neighbors.T, degree, boundary.transpose(1, 0, 2), upstream)
    args = tuple(pltpu.with_memory_space_constraint(arg, pltpu.HBM) for arg in args)
    hidden, node, gathered = pl.pallas_call(
        functools.partial(kernel, inner, outer, levels, bnd),
        out_shape=(
            pltpu.VMEM((nodes, width), bf16),
            pltpu.VMEM((nodes, width), bf16),
            pltpu.VMEM((2 * width, width), bf16),
        ),
        in_specs=[hbm] * 7,
        out_specs=(vmem, vmem, vmem),
        scratch_shapes=[pltpu.VMEM(arg.shape, arg.dtype) for arg in args] + [
            sem((7,)),
            pltpu.VMEM((nodes + rows, nodes), bf16),
            pltpu.VMEM((nodes, rows), bf16),
            pltpu.VMEM((nodes, rows), bf16),
            pltpu.VMEM((rows, width), bf16),
            pltpu.VMEM((rows, width), bf16),
            pltpu.VMEM((rows, width), bf16),
            pltpu.VMEM((rows, width), bf16),
            pltpu.VMEM((2, width, width), bf16),
            pltpu.VMEM((2, inner, chunk, width), bf16),
            pltpu.VMEM((2, chunk, width), bf16),
            pltpu.VMEM((2, outer, chunk, width), bf16),
            sem((levels,)), sem((levels,)), sem((levels,)), sem((levels,)),
            sem((2, inner)), sem((2, inner)), sem((2, outer)), sem((2, outer)), sem((2, inner)), sem((2, inner)),
        ],
        compiler_params=pltpu.CompilerParams(
            collective_id=0, has_side_effects=True, vmem_limit_bytes=40 << 20
        ),
        cost_estimate=pl.CostEstimate(flops=1 << 30, bytes_accessed=3 << 20, transcendentals=nodes * width),
    )(*args)
    return pl.pallas_call(
        finish,
        out_shape=(
            jax.ShapeDtypeStruct((nodes, width), bf16),
            jax.ShapeDtypeStruct((nodes, width), bf16),
            jax.ShapeDtypeStruct((2 * width, width), jnp.float32),
        ),
        in_specs=[vmem] * 3,
        out_specs=(hbm, hbm, hbm),
        scratch_shapes=[pltpu.VMEM((2 * width, width), jnp.float32), sem((3,))],
        compiler_params=pltpu.CompilerParams(vmem_limit_bytes=16 << 20),
        cost_estimate=pl.CostEstimate(flops=1 << 18, bytes_accessed=1 << 20, transcendentals=0),
    )(hidden, node, gathered)


def solution(mesh):
    return jax.shard_map(
        per_device,
        mesh=mesh,
        in_specs=(
            P("dom", None),
            P(),
            P(),
            P("dom", None),
            P("dom"),
            P("dom", None, None),
            P("dom", None),
        ),
        out_specs=(P("dom", None), P("dom", None), P()),
        check_vma=False,
    )
```

```python
import functools

import jax
import jax.numpy as jnp
from jax import lax
from jax.experimental import pallas as pl
from jax.experimental.pallas import tpu as pltpu
from jax.sharding import PartitionSpec as P

epsilon = 1e-06
INNER_BITS = 3
BUILD_ROWS = 128


def partner(me, mask):
    other = me
    bit = 0
    while mask >> bit:
        if (mask >> bit) & 1:
            size = 1 << bit
            other = other + size * (1 - 2 * lax.rem(lax.div(me, size), 2))
        bit += 1
    return other


def dot(a, b):
    return jnp.dot(a, b, preferred_element_type=jnp.float32)


def dot_rows(a, b):
    return lax.dot_general(a, b, (((0,), (0,)), ((), ())), preferred_element_type=jnp.float32)


def dot_cols(a, b):
    return lax.dot_general(a, b, (((1,), (1,)), ((), ())), preferred_element_type=jnp.float32)


def kernel(
    inner, outer, levels, bnd,
    feat_hbm, w_self_hbm, w_neigh_hbm, slots_hbm, degree_hbm, boundary_hbm, up_hbm,
    hidden_ref, node_ref, gathered,
    feat_ref, w_self_ref, w_neigh_ref, slots_ref, degree_ref, boundary_ref, up_ref, fetch_sem,
    table, table_t, pick, out_rows, in_rows, out_grads, in_grads,
    stack, part_in, part, plane_in,
    row_ss, row_rs, grad_ss, grad_rs, part_ss, part_rs, plane_ss, plane_rs, gather_ss, gather_rs,
):
    me = lax.axis_index("dom")
    nodes = feat_ref.shape[0]
    slot_count = slots_ref.shape[0]
    total_rows = table.shape[0]
    chunk = stack.shape[1] // inner
    mine = lax.rem(me, inner)

    fetches = [
        pltpu.make_async_copy(src, dst, fetch_sem.at[index])
        for index, (src, dst) in enumerate((
            (boundary_hbm, boundary_ref), (feat_hbm, feat_ref), (degree_hbm, degree_ref),
            (slots_hbm, slots_ref), (w_self_hbm, w_self_ref), (w_neigh_hbm, w_neigh_ref),
            (up_hbm, up_ref),
        ))
    ]
    for fetch in fetches:
        fetch.start()

    inner_masks = list(range(1, inner))
    outer_masks = [e * inner for e in range(1, outer)]
    barrier = pltpu.get_barrier_semaphore()
    greeted = [1 << level for level in range(levels)]
    greeted += [mask for mask in inner_masks + outer_masks if mask.bit_count() > 2]
    for mask in greeted:
        pl.semaphore_signal(
            barrier, inc=1, device_id=(partner(me, mask),), device_id_type=pl.DeviceIdType.MESH
        )

    def remote(src, dst, send_sem, recv_sem, mask):
        return pltpu.make_async_remote_copy(
            src_ref=src, dst_ref=dst, send_sem=send_sem, recv_sem=recv_sem,
            device_id=(partner(me, mask),), device_id_type=pl.DeviceIdType.MESH,
        )

    fetches[0].wait()
    fetches[1].wait()
    feat = feat_ref[...]

    row_id = lax.broadcasted_iota(jnp.int32, (nodes, bnd), 0)
    row_copies = [None] * levels
    for place, level in enumerate(reversed(range(levels))):
        hot = (row_id == boundary_ref[level]).astype(jnp.float32).astype(jnp.bfloat16)
        span = pl.ds(level * bnd, bnd)
        pick[:, span] = hot
        out_rows[span, :] = dot_rows(hot, feat).astype(jnp.bfloat16)
        if place == 0:
            pl.semaphore_wait(barrier, len(greeted))
        row_copies[level] = remote(
            out_rows.at[span, :], in_rows.at[span, :], row_ss.at[level], row_rs.at[level], 1 << level
        )
        row_copies[level].start()

    fetches[2].wait()
    fetches[3].wait()
    degree_row = degree_ref[...].reshape(1, nodes)
    named = [
        jnp.where(degree_row > slot, slots_ref[slot : slot + 1, :], -1) for slot in range(slot_count)
    ]

    named = jnp.concatenate(named, axis=0).astype(jnp.float32)
    row = lax.broadcasted_iota(jnp.int32, (BUILD_ROWS, nodes), 0).astype(jnp.float32).astype(jnp.bfloat16)

    def build(block, carry):
        start = pl.multiple_of(block * BUILD_ROWS, BUILD_ROWS)
        shifted = (named - start.astype(jnp.float32)).astype(jnp.bfloat16)
        count = jnp.zeros((BUILD_ROWS, nodes), jnp.bfloat16)
        for slot in range(slot_count):
            count = jnp.where(row == shifted[slot : slot + 1, :], count + 1, count)
        table[pl.ds(start, BUILD_ROWS), :] = count
        return carry

    lax.fori_loop(0, total_rows // BUILD_ROWS, build, 0)

    share_row = 1.0 / degree_row.astype(jnp.float32)
    share = jnp.transpose(jnp.broadcast_to(share_row, (128, nodes)))
    share = jnp.concatenate([share] * (feat.shape[1] // 128), axis=1)

    table_t[...] = jnp.transpose(table[nodes:, :])
    feat_t = jnp.transpose(feat)
    summed = dot_rows(table[:nodes, :], feat)
    for fetch in fetches[4:]:
        fetch.wait()
    pre_self = dot(feat, w_self_ref[...])
    inner_levels = inner.bit_length() - 1
    near = inner_levels * bnd
    for level in range(inner_levels):
        row_copies[level].wait_recv()
    summed = summed + dot(table_t[:, :near], in_rows[:near, :])
    for level in range(inner_levels, levels):
        row_copies[level].wait_recv()
    summed = summed + dot(table_t[:, near:], in_rows[near:, :])
    agg = (summed * share).astype(jnp.bfloat16)
    pre_sum = pre_self + dot(agg, w_neigh_ref[...])
    sigmoid = jax.nn.sigmoid(pre_sum)
    hidden_ref[...] = (pre_sum * sigmoid).astype(jnp.bfloat16)
    pre_grad = (
        up_ref[...].astype(jnp.float32) * sigmoid * (1.0 + pre_sum * (1.0 - sigmoid))
    ).astype(jnp.bfloat16)

    width = feat.shape[1]
    part_copies = []
    for half in range(2):
        left_t = feat_t if half == 0 else jnp.transpose(agg)
        stack[half] = dot(left_t, pre_grad).astype(jnp.bfloat16)
        for mask in inner_masks:
            theirs = lax.rem(partner(me, mask), inner)
            copy = remote(
                stack.at[half, pl.ds(pl.multiple_of(theirs * chunk, chunk), chunk), :],
                part_in.at[half, mask], part_ss.at[half, mask], part_rs.at[half, mask], mask,
            )
            copy.start()
            part_copies.append(copy)

    slot_share = (dot_cols(pre_grad, w_neigh_ref[...]) * share).astype(jnp.bfloat16)
    out_grads[...] = dot(table[nodes:, :], slot_share).astype(jnp.bfloat16)
    grad_copies = []

    def return_grads(level):
        span = pl.ds(level * bnd, bnd)
        copy = remote(
            out_grads.at[span, :], in_grads.at[span, :], grad_ss.at[level], grad_rs.at[level], 1 << level
        )
        copy.start()
        grad_copies.append(copy)

    for level in reversed(range(levels)):
        return_grads(level)
    local = dot_cols(pre_grad, w_self_ref[...]) + dot(table[:nodes, :], slot_share)

    own = pl.ds(pl.multiple_of(mine * chunk, chunk), chunk)
    per_half = len(inner_masks)
    plane_copies = []
    for half in range(2):
        for copy in part_copies[half * per_half : (half + 1) * per_half]:
            copy.wait_recv()
        total = stack[half, own, :].astype(jnp.float32)
        for mask in inner_masks:
            total = total + part_in[half, mask].astype(jnp.float32)
        part[half] = total.astype(jnp.bfloat16)
        for index, mask in enumerate(outer_masks):
            copy = remote(
                part.at[half], plane_in.at[half, index + 1],
                plane_ss.at[half, index + 1], plane_rs.at[half, index + 1], mask,
            )
            copy.start()
            plane_copies.append(copy)

    per_outer = len(outer_masks)
    gather_copies = []
    for half in range(2):
        for copy in plane_copies[half * per_outer : (half + 1) * per_outer]:
            copy.wait_recv()
        terms = [part[half].astype(jnp.float32)]
        for index in range(1, outer):
            terms.append(plane_in[half, index].astype(jnp.float32))
        while len(terms) > 1:
            terms = [terms[i] + terms[i + 1] for i in range(0, len(terms), 2)]
        rows = pl.ds(pl.multiple_of(half * width + mine * chunk, chunk), chunk)
        gathered[rows, :] = terms[0].astype(jnp.bfloat16)
        for mask in inner_masks:
            copy = remote(
                gathered.at[rows, :], gathered.at[rows, :],
                gather_ss.at[half, mask], gather_rs.at[half, mask], mask,
            )
            copy.start()
            gather_copies.append(copy)

    for copy in grad_copies:
        copy.wait_recv()
    node_ref[...] = (local + dot(pick[...], in_grads[...])).astype(jnp.bfloat16)
    for copy in gather_copies:
        copy.wait_recv()

    for copy in row_copies + part_copies + grad_copies + plane_copies + gather_copies:
        copy.wait_send()


def finish(hidden, node, gathered, hidden_hbm, node_hbm, step_hbm, step, sems):
    copies = [
        pltpu.make_async_copy(hidden, hidden_hbm, sems.at[0]),
        pltpu.make_async_copy(node, node_hbm, sems.at[1]),
        pltpu.make_async_copy(step, step_hbm, sems.at[2]),
    ]
    copies[0].start()
    copies[1].start()
    whole = gathered[...].astype(jnp.float32)
    step[...] = whole * lax.rsqrt(jnp.mean(whole * whole) + epsilon)
    copies[2].start()
    for copy in copies:
        copy.wait()


def per_device(features, w_self, w_neigh, neighbors, degree, boundary, upstream):
    size = lax.axis_size("dom")
    levels = size.bit_length() - 1
    inner = min(size, 1 << INNER_BITS)
    outer = size // inner
    nodes, width = features.shape
    bnd = boundary.shape[2]
    rows = levels * bnd
    chunk = width // inner
    bf16 = jnp.bfloat16
    sem = pltpu.SemaphoreType.DMA
    vmem = pl.BlockSpec(memory_space=pltpu.VMEM)
    hbm = pl.BlockSpec(memory_space=pltpu.HBM)
    args = (features, w_self, w_neigh, neighbors.T, degree, boundary.transpose(1, 0, 2), upstream)
    args = tuple(pltpu.with_memory_space_constraint(arg, pltpu.HBM) for arg in args)
    hidden, node, gathered = pl.pallas_call(
        functools.partial(kernel, inner, outer, levels, bnd),
        out_shape=(
            pltpu.VMEM((nodes, width), bf16),
            pltpu.VMEM((nodes, width), bf16),
            pltpu.VMEM((2 * width, width), bf16),
        ),
        in_specs=[hbm] * 7,
        out_specs=(vmem, vmem, vmem),
        scratch_shapes=[pltpu.VMEM(arg.shape, arg.dtype) for arg in args] + [
            sem((7,)),
            pltpu.VMEM((nodes + rows, nodes), bf16),
            pltpu.VMEM((nodes, rows), bf16),
            pltpu.VMEM((nodes, rows), bf16),
            pltpu.VMEM((rows, width), bf16),
            pltpu.VMEM((rows, width), bf16),
            pltpu.VMEM((rows, width), bf16),
            pltpu.VMEM((rows, width), bf16),
            pltpu.VMEM((2, width, width), bf16),
            pltpu.VMEM((2, inner, chunk, width), bf16),
            pltpu.VMEM((2, chunk, width), bf16),
            pltpu.VMEM((2, outer, chunk, width), bf16),
            sem((levels,)), sem((levels,)), sem((levels,)), sem((levels,)),
            sem((2, inner)), sem((2, inner)), sem((2, outer)), sem((2, outer)), sem((2, inner)), sem((2, inner)),
        ],
        compiler_params=pltpu.CompilerParams(
            collective_id=0, has_side_effects=True, vmem_limit_bytes=40 << 20
        ),
        cost_estimate=pl.CostEstimate(flops=1 << 30, bytes_accessed=3 << 20, transcendentals=nodes * width),
    )(*args)
    return pl.pallas_call(
        finish,
        out_shape=(
            jax.ShapeDtypeStruct((nodes, width), bf16),
            jax.ShapeDtypeStruct((nodes, width), bf16),
            jax.ShapeDtypeStruct((2 * width, width), jnp.float32),
        ),
        in_specs=[vmem] * 3,
        out_specs=(hbm, hbm, hbm),
        scratch_shapes=[pltpu.VMEM((2 * width, width), jnp.float32), sem((3,))],
        compiler_params=pltpu.CompilerParams(vmem_limit_bytes=16 << 20),
        cost_estimate=pl.CostEstimate(flops=1 << 18, bytes_accessed=1 << 20, transcendentals=0),
    )(hidden, node, gathered)


def solution(mesh):
    return jax.shard_map(
        per_device,
        mesh=mesh,
        in_specs=(
            P("dom", None),
            P(),
            P(),
            P("dom", None),
            P("dom"),
            P("dom", None, None),
            P("dom", None),
        ),
        out_specs=(P("dom", None), P("dom", None), P()),
        check_vma=False,
    )
```

```python
import functools

import jax
import jax.numpy as jnp
from jax import lax
from jax.experimental import pallas as pl
from jax.experimental.pallas import tpu as pltpu
from jax.sharding import PartitionSpec as P

epsilon = 1e-06
INNER_BITS = 3
BUILD_ROWS = 128


def partner(me, mask):
    other = me
    bit = 0
    while mask >> bit:
        if (mask >> bit) & 1:
            size = 1 << bit
            other = other + size * (1 - 2 * lax.rem(lax.div(me, size), 2))
        bit += 1
    return other


def dot(a, b):
    return jnp.dot(a, b, preferred_element_type=jnp.float32)


def dot_rows(a, b):
    return lax.dot_general(a, b, (((0,), (0,)), ((), ())), preferred_element_type=jnp.float32)


def dot_cols(a, b):
    return lax.dot_general(a, b, (((1,), (1,)), ((), ())), preferred_element_type=jnp.float32)


def kernel(
    inner, outer, levels, bnd,
    feat_hbm, w_self_hbm, w_neigh_hbm, slots_hbm, degree_hbm, boundary_hbm, up_hbm,
    hidden_ref, node_ref, gathered,
    feat_ref, w_self_ref, w_neigh_ref, slots_ref, degree_ref, boundary_ref, up_ref, fetch_sem,
    feat_t, table, pick, out_rows, in_rows, out_grads, in_grads,
    stack, part_in, part, plane_in,
    row_ss, row_rs, grad_ss, grad_rs, part_ss, part_rs, plane_ss, plane_rs, gather_ss, gather_rs,
):
    me = lax.axis_index("dom")
    nodes = feat_ref.shape[0]
    slot_count = slots_ref.shape[0]
    total_rows = table.shape[0]
    chunk = stack.shape[1] // inner
    mine = lax.rem(me, inner)

    fetches = [
        pltpu.make_async_copy(src, dst, fetch_sem.at[index])
        for index, (src, dst) in enumerate((
            (boundary_hbm, boundary_ref), (feat_hbm, feat_ref), (degree_hbm, degree_ref),
            (slots_hbm, slots_ref), (w_self_hbm, w_self_ref), (w_neigh_hbm, w_neigh_ref),
            (up_hbm, up_ref),
        ))
    ]
    for fetch in fetches:
        fetch.start()

    inner_masks = list(range(1, inner))
    outer_masks = [e * inner for e in range(1, outer)]
    barrier = pltpu.get_barrier_semaphore()
    greeted = [1 << level for level in range(levels)]
    greeted += [mask for mask in inner_masks + outer_masks if mask.bit_count() > 2]
    for mask in greeted:
        pl.semaphore_signal(
            barrier, inc=1, device_id=(partner(me, mask),), device_id_type=pl.DeviceIdType.MESH
        )

    def remote(src, dst, send_sem, recv_sem, mask):
        return pltpu.make_async_remote_copy(
            src_ref=src, dst_ref=dst, send_sem=send_sem, recv_sem=recv_sem,
            device_id=(partner(me, mask),), device_id_type=pl.DeviceIdType.MESH,
        )

    fetches[0].wait()
    fetches[1].wait()
    feat_t[...] = jnp.transpose(feat_ref[...])

    row_id = lax.broadcasted_iota(jnp.int32, (nodes, bnd), 0)
    for level in range(levels):
        hot = (row_id == boundary_ref[level]).astype(jnp.float32).astype(jnp.bfloat16)
        pick[:, pl.ds(level * bnd, bnd)] = hot
    picked = dot(feat_t[...], pick[...]).astype(jnp.bfloat16)
    for level in range(levels):
        out_rows[level] = picked[:, level * bnd : (level + 1) * bnd]
    pl.semaphore_wait(barrier, len(greeted))
    row_copies = [
        remote(out_rows.at[level], in_rows.at[level], row_ss.at[level], row_rs.at[level], 1 << level)
        for level in range(levels)
    ]
    for copy in reversed(row_copies):
        copy.start()

    fetches[2].wait()
    fetches[3].wait()
    degree_row = degree_ref[...].reshape(1, nodes)
    named = [
        jnp.where(degree_row > slot, slots_ref[slot : slot + 1, :], -1) for slot in range(slot_count)
    ]

    named = jnp.concatenate(named, axis=0).astype(jnp.float32)
    row = lax.broadcasted_iota(jnp.int32, (BUILD_ROWS, nodes), 0).astype(jnp.float32).astype(jnp.bfloat16)

    def build(block, carry):
        start = pl.multiple_of(block * BUILD_ROWS, BUILD_ROWS)
        shifted = (named - start.astype(jnp.float32)).astype(jnp.bfloat16)
        count = jnp.zeros((BUILD_ROWS, nodes), jnp.bfloat16)
        for slot in range(slot_count):
            count = jnp.where(row == shifted[slot : slot + 1, :], count + 1, count)
        table[pl.ds(start, BUILD_ROWS), :] = count
        return carry

    lax.fori_loop(0, total_rows // BUILD_ROWS, build, 0)

    share = 1.0 / degree_row.astype(jnp.float32)
    summed = dot(feat_t[...], table[:nodes, :])
    for fetch in fetches[4:]:
        fetch.wait()
    pre_self = dot_rows(w_self_ref[...], feat_t[...])
    w_neigh_t = jnp.transpose(w_neigh_ref[...])
    up_t = jnp.transpose(up_ref[...])

    inner_levels = inner.bit_length() - 1
    for low, high in ((0, inner_levels), (inner_levels, levels)):
        for level in range(low, high):
            row_copies[level].wait_recv()
        rows_t = jnp.concatenate([in_rows[level] for level in range(low, high)], axis=1)
        summed = summed + dot(rows_t, table[nodes + low * bnd : nodes + high * bnd, :])
    agg_t = (summed * share).astype(jnp.bfloat16)
    pre_sum = pre_self + dot(w_neigh_t, agg_t)
    sigmoid = jax.nn.sigmoid(pre_sum)
    pre_grad = (
        up_t.astype(jnp.float32) * sigmoid * (1.0 + pre_sum * (1.0 - sigmoid))
    ).astype(jnp.bfloat16)

    width = feat_t.shape[0]
    part_copies = []
    for half in range(2):
        left_t = feat_t[...] if half == 0 else agg_t
        stack[half] = dot_cols(left_t, pre_grad).astype(jnp.bfloat16)
        for mask in inner_masks:
            theirs = lax.rem(partner(me, mask), inner)
            copy = remote(
                stack.at[half, pl.ds(pl.multiple_of(theirs * chunk, chunk), chunk), :],
                part_in.at[half, mask], part_ss.at[half, mask], part_rs.at[half, mask], mask,
            )
            copy.start()
            part_copies.append(copy)

    slot_share = (dot(w_neigh_ref[...], pre_grad) * share).astype(jnp.bfloat16)
    out_grads[...] = dot_cols(table[nodes:, :], slot_share).astype(jnp.bfloat16)
    grad_copies = []

    def return_grads(level):
        span = pl.ds(level * bnd, bnd)
        copy = remote(
            out_grads.at[span, :], in_grads.at[span, :], grad_ss.at[level], grad_rs.at[level], 1 << level
        )
        copy.start()
        grad_copies.append(copy)

    for level in reversed(range(levels)):
        return_grads(level)
    hidden_ref[...] = jnp.transpose((pre_sum * sigmoid).astype(jnp.bfloat16))
    local = jnp.transpose(dot(w_self_ref[...], pre_grad)) + dot_cols(table[:nodes, :], slot_share)

    own = pl.ds(pl.multiple_of(mine * chunk, chunk), chunk)
    per_half = len(inner_masks)
    plane_copies = []
    for half in range(2):
        for copy in part_copies[half * per_half : (half + 1) * per_half]:
            copy.wait_recv()
        total = stack[half, own, :].astype(jnp.float32)
        for mask in inner_masks:
            total = total + part_in[half, mask].astype(jnp.float32)
        part[half] = total.astype(jnp.bfloat16)
        for index, mask in enumerate(outer_masks):
            copy = remote(
                part.at[half], plane_in.at[half, index + 1],
                plane_ss.at[half, index + 1], plane_rs.at[half, index + 1], mask,
            )
            copy.start()
            plane_copies.append(copy)

    per_outer = len(outer_masks)
    gather_copies = []
    for half in range(2):
        for copy in plane_copies[half * per_outer : (half + 1) * per_outer]:
            copy.wait_recv()
        terms = [part[half].astype(jnp.float32)]
        for index in range(1, outer):
            terms.append(plane_in[half, index].astype(jnp.float32))
        while len(terms) > 1:
            terms = [terms[i] + terms[i + 1] for i in range(0, len(terms), 2)]
        rows = pl.ds(pl.multiple_of(half * width + mine * chunk, chunk), chunk)
        gathered[rows, :] = terms[0].astype(jnp.bfloat16)
        for mask in inner_masks:
            copy = remote(
                gathered.at[rows, :], gathered.at[rows, :],
                gather_ss.at[half, mask], gather_rs.at[half, mask], mask,
            )
            copy.start()
            gather_copies.append(copy)

    for copy in grad_copies:
        copy.wait_recv()
    node_ref[...] = (local + dot(pick[...], in_grads[...])).astype(jnp.bfloat16)
    for copy in gather_copies:
        copy.wait_recv()

    for copy in row_copies + part_copies + grad_copies + plane_copies + gather_copies:
        copy.wait_send()


def finish(hidden, node, gathered, hidden_hbm, node_hbm, step_hbm, step, sems):
    copies = [
        pltpu.make_async_copy(hidden, hidden_hbm, sems.at[0]),
        pltpu.make_async_copy(node, node_hbm, sems.at[1]),
        pltpu.make_async_copy(step, step_hbm, sems.at[2]),
    ]
    copies[0].start()
    copies[1].start()
    whole = gathered[...].astype(jnp.float32)
    step[...] = whole * lax.rsqrt(jnp.mean(whole * whole) + epsilon)
    copies[2].start()
    for copy in copies:
        copy.wait()


def per_device(features, w_self, w_neigh, neighbors, degree, boundary, upstream):
    size = lax.axis_size("dom")
    levels = size.bit_length() - 1
    inner = min(size, 1 << INNER_BITS)
    outer = size // inner
    nodes, width = features.shape
    bnd = boundary.shape[2]
    rows = levels * bnd
    chunk = width // inner
    bf16 = jnp.bfloat16
    sem = pltpu.SemaphoreType.DMA
    vmem = pl.BlockSpec(memory_space=pltpu.VMEM)
    hbm = pl.BlockSpec(memory_space=pltpu.HBM)
    args = (features, w_self, w_neigh, neighbors.T, degree, boundary.transpose(1, 0, 2), upstream)
    args = tuple(pltpu.with_memory_space_constraint(arg, pltpu.HBM) for arg in args)
    hidden, node, gathered = pl.pallas_call(
        functools.partial(kernel, inner, outer, levels, bnd),
        out_shape=(
            pltpu.VMEM((nodes, width), bf16),
            pltpu.VMEM((nodes, width), bf16),
            pltpu.VMEM((2 * width, width), bf16),
        ),
        in_specs=[hbm] * 7,
        out_specs=(vmem, vmem, vmem),
        scratch_shapes=[pltpu.VMEM(arg.shape, arg.dtype) for arg in args] + [
            sem((7,)),
            pltpu.VMEM((width, nodes), bf16),
            pltpu.VMEM((nodes + rows, nodes), bf16),
            pltpu.VMEM((nodes, rows), bf16),
            pltpu.VMEM((levels, width, bnd), bf16),
            pltpu.VMEM((levels, width, bnd), bf16),
            pltpu.VMEM((rows, width), bf16),
            pltpu.VMEM((rows, width), bf16),
            pltpu.VMEM((2, width, width), bf16),
            pltpu.VMEM((2, inner, chunk, width), bf16),
            pltpu.VMEM((2, chunk, width), bf16),
            pltpu.VMEM((2, outer, chunk, width), bf16),
            sem((levels,)), sem((levels,)), sem((levels,)), sem((levels,)),
            sem((2, inner)), sem((2, inner)), sem((2, outer)), sem((2, outer)), sem((2, inner)), sem((2, inner)),
        ],
        compiler_params=pltpu.CompilerParams(
            collective_id=0, has_side_effects=True, vmem_limit_bytes=40 << 20
        ),
        cost_estimate=pl.CostEstimate(flops=1 << 30, bytes_accessed=3 << 20, transcendentals=nodes * width),
    )(*args)
    return pl.pallas_call(
        finish,
        out_shape=(
            jax.ShapeDtypeStruct((nodes, width), bf16),
            jax.ShapeDtypeStruct((nodes, width), bf16),
            jax.ShapeDtypeStruct((2 * width, width), jnp.float32),
        ),
        in_specs=[vmem] * 3,
        out_specs=(hbm, hbm, hbm),
        scratch_shapes=[pltpu.VMEM((2 * width, width), jnp.float32), sem((3,))],
        compiler_params=pltpu.CompilerParams(vmem_limit_bytes=16 << 20),
        cost_estimate=pl.CostEstimate(flops=1 << 18, bytes_accessed=1 << 20, transcendentals=0),
    )(hidden, node, gathered)


def solution(mesh):
    return jax.shard_map(
        per_device,
        mesh=mesh,
        in_specs=(
            P("dom", None),
            P(),
            P(),
            P("dom", None),
            P("dom"),
            P("dom", None, None),
            P("dom", None),
        ),
        out_specs=(P("dom", None), P("dom", None), P()),
        check_vma=False,
    )
```

```python
import functools

import jax
import jax.numpy as jnp
from jax import lax
from jax.experimental import pallas as pl
from jax.experimental.pallas import tpu as pltpu
from jax.sharding import PartitionSpec as P

epsilon = 1e-06
INNER_BITS = 3
BUILD_ROWS = 128


def partner(me, mask):
    other = me
    bit = 0
    while mask >> bit:
        if (mask >> bit) & 1:
            size = 1 << bit
            other = other + size * (1 - 2 * lax.rem(lax.div(me, size), 2))
        bit += 1
    return other


def dot(a, b):
    return jnp.dot(a, b, preferred_element_type=jnp.float32)


def dot_rows(a, b):
    return lax.dot_general(a, b, (((0,), (0,)), ((), ())), preferred_element_type=jnp.float32)


def dot_cols(a, b):
    return lax.dot_general(a, b, (((1,), (1,)), ((), ())), preferred_element_type=jnp.float32)


def kernel(
    inner, outer, levels, bnd,
    feat_hbm, w_self_hbm, w_neigh_hbm, slots_hbm, degree_hbm, boundary_hbm, up_hbm,
    hidden_ref, node_ref, gathered,
    feat_ref, w_self_ref, w_neigh_ref, slots_ref, degree_ref, boundary_ref, up_ref, fetch_sem,
    feat_t, table, pick, out_rows, in_rows, out_grads, in_grads,
    stack, part_in, part, plane_in,
    row_ss, row_rs, grad_ss, grad_rs, part_ss, part_rs, plane_ss, plane_rs, gather_ss, gather_rs,
):
    me = lax.axis_index("dom")
    nodes = feat_ref.shape[0]
    slot_count = slots_ref.shape[0]
    total_rows = table.shape[0]
    chunk = stack.shape[1] // inner
    mine = lax.rem(me, inner)

    fetches = [
        pltpu.make_async_copy(src, dst, fetch_sem.at[index])
        for index, (src, dst) in enumerate((
            (boundary_hbm, boundary_ref), (feat_hbm, feat_ref), (degree_hbm, degree_ref),
            (slots_hbm, slots_ref), (w_self_hbm, w_self_ref), (w_neigh_hbm, w_neigh_ref),
            (up_hbm, up_ref),
        ))
    ]
    for fetch in fetches:
        fetch.start()

    inner_masks = list(range(inner - 1, 0, -1))
    outer_masks = [e * inner for e in range(outer - 1, 0, -1)]
    barrier = pltpu.get_barrier_semaphore()
    greeted = [1 << level for level in range(levels)]
    greeted += [mask for mask in inner_masks + outer_masks if mask.bit_count() > 2]
    for mask in greeted:
        pl.semaphore_signal(
            barrier, inc=1, device_id=(partner(me, mask),), device_id_type=pl.DeviceIdType.MESH
        )

    def remote(src, dst, send_sem, recv_sem, mask):
        return pltpu.make_async_remote_copy(
            src_ref=src, dst_ref=dst, send_sem=send_sem, recv_sem=recv_sem,
            device_id=(partner(me, mask),), device_id_type=pl.DeviceIdType.MESH,
        )

    fetches[0].wait()
    fetches[1].wait()
    feat_t[...] = jnp.transpose(feat_ref[...])

    row_id = lax.broadcasted_iota(jnp.int32, (nodes, bnd), 0)
    for level in range(levels):
        hot = (row_id == boundary_ref[level]).astype(jnp.float32).astype(jnp.bfloat16)
        pick[:, pl.ds(level * bnd, bnd)] = hot
    picked = dot(feat_t[...], pick[...]).astype(jnp.bfloat16)
    for level in range(levels):
        out_rows[level] = picked[:, level * bnd : (level + 1) * bnd]
    pl.semaphore_wait(barrier, len(greeted))
    row_copies = [
        remote(out_rows.at[level], in_rows.at[level], row_ss.at[level], row_rs.at[level], 1 << level)
        for level in range(levels)
    ]
    for copy in reversed(row_copies):
        copy.start()

    fetches[2].wait()
    fetches[3].wait()
    degree_row = degree_ref[...].reshape(1, nodes)
    named = [
        jnp.where(degree_row > slot, slots_ref[slot : slot + 1, :], -1) for slot in range(slot_count)
    ]

    named = jnp.concatenate(named, axis=0).astype(jnp.float32)
    row = lax.broadcasted_iota(jnp.int32, (BUILD_ROWS, nodes), 0).astype(jnp.float32).astype(jnp.bfloat16)

    def build(block, carry):
        start = pl.multiple_of(block * BUILD_ROWS, BUILD_ROWS)
        shifted = (named - start.astype(jnp.float32)).astype(jnp.bfloat16)
        count = jnp.zeros((BUILD_ROWS, nodes), jnp.bfloat16)
        for slot in range(slot_count):
            count = jnp.where(row == shifted[slot : slot + 1, :], count + 1, count)
        table[pl.ds(start, BUILD_ROWS), :] = count
        return carry

    lax.fori_loop(0, total_rows // BUILD_ROWS, build, 0)

    share = 1.0 / degree_row.astype(jnp.float32)
    summed = dot(feat_t[...], table[:nodes, :])
    for fetch in fetches[4:]:
        fetch.wait()
    pre_self = dot_rows(w_self_ref[...], feat_t[...])
    w_neigh_t = jnp.transpose(w_neigh_ref[...])
    up_t = jnp.transpose(up_ref[...])

    inner_levels = inner.bit_length() - 1
    for low, high in ((0, inner_levels), (inner_levels, levels)):
        for level in range(low, high):
            row_copies[level].wait_recv()
        rows_t = jnp.concatenate([in_rows[level] for level in range(low, high)], axis=1)
        summed = summed + dot(rows_t, table[nodes + low * bnd : nodes + high * bnd, :])
    agg_t = (summed * share).astype(jnp.bfloat16)
    pre_sum = pre_self + dot(w_neigh_t, agg_t)
    sigmoid = jax.nn.sigmoid(pre_sum)
    pre_grad = (
        up_t.astype(jnp.float32) * sigmoid * (1.0 + pre_sum * (1.0 - sigmoid))
    ).astype(jnp.bfloat16)

    width = feat_t.shape[0]
    part_copies = []
    for half in range(2):
        left_t = feat_t[...] if half == 0 else agg_t
        stack[half] = dot_cols(left_t, pre_grad).astype(jnp.bfloat16)
        for mask in inner_masks:
            theirs = lax.rem(partner(me, mask), inner)
            copy = remote(
                stack.at[half, pl.ds(pl.multiple_of(theirs * chunk, chunk), chunk), :],
                part_in.at[half, mask], part_ss.at[half, mask], part_rs.at[half, mask], mask,
            )
            copy.start()
            part_copies.append(copy)

    slot_share = (dot(w_neigh_ref[...], pre_grad) * share).astype(jnp.bfloat16)
    out_grads[...] = dot_cols(table[nodes:, :], slot_share).astype(jnp.bfloat16)
    grad_copies = []

    def return_grads(level):
        span = pl.ds(level * bnd, bnd)
        copy = remote(
            out_grads.at[span, :], in_grads.at[span, :], grad_ss.at[level], grad_rs.at[level], 1 << level
        )
        copy.start()
        grad_copies.append(copy)

    for level in reversed(range(inner_levels, levels)):
        return_grads(level)
    hidden_ref[...] = jnp.transpose((pre_sum * sigmoid).astype(jnp.bfloat16))
    local = jnp.transpose(dot(w_self_ref[...], pre_grad)) + dot_cols(table[:nodes, :], slot_share)

    own = pl.ds(pl.multiple_of(mine * chunk, chunk), chunk)
    per_half = len(inner_masks)
    plane_copies = []
    for half in range(2):
        for copy in part_copies[half * per_half : (half + 1) * per_half]:
            copy.wait_recv()
        total = stack[half, own, :].astype(jnp.float32)
        for mask in inner_masks:
            total = total + part_in[half, mask].astype(jnp.float32)
        part[half] = total.astype(jnp.bfloat16)
        for mask in outer_masks:
            index = mask // inner
            copy = remote(
                part.at[half], plane_in.at[half, index],
                plane_ss.at[half, index], plane_rs.at[half, index], mask,
            )
            copy.start()
            plane_copies.append(copy)

    for level in reversed(range(inner_levels)):
        return_grads(level)

    per_outer = len(outer_masks)
    gather_copies = []
    for half in range(2):
        for copy in plane_copies[half * per_outer : (half + 1) * per_outer]:
            copy.wait_recv()
        terms = [part[half].astype(jnp.float32)]
        for index in range(1, outer):
            terms.append(plane_in[half, index].astype(jnp.float32))
        while len(terms) > 1:
            terms = [terms[i] + terms[i + 1] for i in range(0, len(terms), 2)]
        rows = pl.ds(pl.multiple_of(half * width + mine * chunk, chunk), chunk)
        gathered[rows, :] = terms[0].astype(jnp.bfloat16)
        for mask in inner_masks:
            copy = remote(
                gathered.at[rows, :], gathered.at[rows, :],
                gather_ss.at[half, mask], gather_rs.at[half, mask], mask,
            )
            copy.start()
            gather_copies.append(copy)

    for copy in grad_copies:
        copy.wait_recv()
    node_ref[...] = (local + dot(pick[...], in_grads[...])).astype(jnp.bfloat16)
    for copy in gather_copies:
        copy.wait_recv()

    for copy in row_copies + part_copies + grad_copies + plane_copies + gather_copies:
        copy.wait_send()


def finish(hidden, node, gathered, hidden_hbm, node_hbm, step_hbm, step, sems):
    copies = [
        pltpu.make_async_copy(hidden, hidden_hbm, sems.at[0]),
        pltpu.make_async_copy(node, node_hbm, sems.at[1]),
        pltpu.make_async_copy(step, step_hbm, sems.at[2]),
    ]
    copies[0].start()
    copies[1].start()
    whole = gathered[...].astype(jnp.float32)
    step[...] = whole * lax.rsqrt(jnp.mean(whole * whole) + epsilon)
    copies[2].start()
    for copy in copies:
        copy.wait()


def per_device(features, w_self, w_neigh, neighbors, degree, boundary, upstream):
    size = lax.axis_size("dom")
    levels = size.bit_length() - 1
    inner = min(size, 1 << INNER_BITS)
    outer = size // inner
    nodes, width = features.shape
    bnd = boundary.shape[2]
    rows = levels * bnd
    chunk = width // inner
    bf16 = jnp.bfloat16
    sem = pltpu.SemaphoreType.DMA
    vmem = pl.BlockSpec(memory_space=pltpu.VMEM)
    hbm = pl.BlockSpec(memory_space=pltpu.HBM)
    args = (features, w_self, w_neigh, neighbors.T, degree, boundary.transpose(1, 0, 2), upstream)
    args = tuple(pltpu.with_memory_space_constraint(arg, pltpu.HBM) for arg in args)
    hidden, node, gathered = pl.pallas_call(
        functools.partial(kernel, inner, outer, levels, bnd),
        out_shape=(
            pltpu.VMEM((nodes, width), bf16),
            pltpu.VMEM((nodes, width), bf16),
            pltpu.VMEM((2 * width, width), bf16),
        ),
        in_specs=[hbm] * 7,
        out_specs=(vmem, vmem, vmem),
        scratch_shapes=[pltpu.VMEM(arg.shape, arg.dtype) for arg in args] + [
            sem((7,)),
            pltpu.VMEM((width, nodes), bf16),
            pltpu.VMEM((nodes + rows, nodes), bf16),
            pltpu.VMEM((nodes, rows), bf16),
            pltpu.VMEM((levels, width, bnd), bf16),
            pltpu.VMEM((levels, width, bnd), bf16),
            pltpu.VMEM((rows, width), bf16),
            pltpu.VMEM((rows, width), bf16),
            pltpu.VMEM((2, width, width), bf16),
            pltpu.VMEM((2, inner, chunk, width), bf16),
            pltpu.VMEM((2, chunk, width), bf16),
            pltpu.VMEM((2, outer, chunk, width), bf16),
            sem((levels,)), sem((levels,)), sem((levels,)), sem((levels,)),
            sem((2, inner)), sem((2, inner)), sem((2, outer)), sem((2, outer)), sem((2, inner)), sem((2, inner)),
        ],
        compiler_params=pltpu.CompilerParams(
            collective_id=0, has_side_effects=True, vmem_limit_bytes=40 << 20
        ),
        cost_estimate=pl.CostEstimate(flops=1 << 30, bytes_accessed=3 << 20, transcendentals=nodes * width),
    )(*args)
    return pl.pallas_call(
        finish,
        out_shape=(
            jax.ShapeDtypeStruct((nodes, width), bf16),
            jax.ShapeDtypeStruct((nodes, width), bf16),
            jax.ShapeDtypeStruct((2 * width, width), jnp.float32),
        ),
        in_specs=[vmem] * 3,
        out_specs=(hbm, hbm, hbm),
        scratch_shapes=[pltpu.VMEM((2 * width, width), jnp.float32), sem((3,))],
        compiler_params=pltpu.CompilerParams(vmem_limit_bytes=16 << 20),
        cost_estimate=pl.CostEstimate(flops=1 << 18, bytes_accessed=1 << 20, transcendentals=0),
    )(hidden, node, gathered)


def solution(mesh):
    return jax.shard_map(
        per_device,
        mesh=mesh,
        in_specs=(
            P("dom", None),
            P(),
            P(),
            P("dom", None),
            P("dom"),
            P("dom", None, None),
            P("dom", None),
        ),
        out_specs=(P("dom", None), P("dom", None), P()),
        check_vma=False,
    )
```

```python
import functools

import jax
import jax.numpy as jnp
from jax import lax
from jax.experimental import pallas as pl
from jax.experimental.pallas import tpu as pltpu
from jax.sharding import PartitionSpec as P

epsilon = 1e-06
INNER_BITS = 3
BUILD_ROWS = 128


def partner(me, mask):
    other = me
    bit = 0
    while mask >> bit:
        if (mask >> bit) & 1:
            size = 1 << bit
            other = other + size * (1 - 2 * lax.rem(lax.div(me, size), 2))
        bit += 1
    return other


def dot(a, b):
    return jnp.dot(a, b, preferred_element_type=jnp.float32)


def dot_rows(a, b):
    return lax.dot_general(a, b, (((0,), (0,)), ((), ())), preferred_element_type=jnp.float32)


def dot_cols(a, b):
    return lax.dot_general(a, b, (((1,), (1,)), ((), ())), preferred_element_type=jnp.float32)


def kernel(
    inner, outer, levels, bnd,
    feat_hbm, w_self_hbm, w_neigh_hbm, slots_hbm, degree_hbm, boundary_hbm, up_hbm,
    hidden_ref, node_ref, gathered,
    feat_ref, w_self_ref, w_neigh_ref, slots_ref, degree_ref, boundary_ref, up_ref, fetch_sem,
    feat_t, table, pick, out_rows, in_rows, out_grads, in_grads,
    stack, part_in, part, plane_in,
    row_ss, row_rs, grad_ss, grad_rs, part_ss, part_rs, plane_ss, plane_rs, gather_ss, gather_rs,
):
    me = lax.axis_index("dom")
    nodes = feat_ref.shape[0]
    slot_count = slots_ref.shape[0]
    total_rows = table.shape[0]
    chunk = stack.shape[1] // inner
    mine = lax.rem(me, inner)

    fetches = [
        pltpu.make_async_copy(src, dst, fetch_sem.at[index])
        for index, (src, dst) in enumerate((
            (boundary_hbm, boundary_ref), (feat_hbm, feat_ref), (degree_hbm, degree_ref),
            (slots_hbm, slots_ref), (w_self_hbm, w_self_ref), (w_neigh_hbm, w_neigh_ref),
            (up_hbm, up_ref),
        ))
    ]
    for fetch in fetches:
        fetch.start()

    inner_masks = list(range(inner - 1, 0, -1))
    outer_masks = [e * inner for e in range(outer - 1, 0, -1)]
    barrier = pltpu.get_barrier_semaphore()
    greeted = [1 << level for level in range(levels)]
    greeted += [mask for mask in inner_masks + outer_masks if mask.bit_count() > 2]
    for mask in greeted:
        pl.semaphore_signal(
            barrier, inc=1, device_id=(partner(me, mask),), device_id_type=pl.DeviceIdType.MESH
        )

    def remote(src, dst, send_sem, recv_sem, mask):
        return pltpu.make_async_remote_copy(
            src_ref=src, dst_ref=dst, send_sem=send_sem, recv_sem=recv_sem,
            device_id=(partner(me, mask),), device_id_type=pl.DeviceIdType.MESH,
        )

    fetches[0].wait()
    fetches[1].wait()
    feat_t[...] = jnp.transpose(feat_ref[...])

    row_id = lax.broadcasted_iota(jnp.int32, (nodes, bnd), 0)
    for level in range(levels):
        hot = (row_id == boundary_ref[level]).astype(jnp.float32).astype(jnp.bfloat16)
        pick[:, pl.ds(level * bnd, bnd)] = hot
    picked = dot(feat_t[...], pick[...]).astype(jnp.bfloat16)
    for level in range(levels):
        out_rows[level] = picked[:, level * bnd : (level + 1) * bnd]
    pl.semaphore_wait(barrier, len(greeted))
    row_copies = [
        remote(out_rows.at[level], in_rows.at[level], row_ss.at[level], row_rs.at[level], 1 << level)
        for level in range(levels)
    ]
    for copy in reversed(row_copies):
        copy.start()

    fetches[2].wait()
    fetches[3].wait()
    degree_row = degree_ref[...].reshape(1, nodes)
    named = [
        jnp.where(degree_row > slot, slots_ref[slot : slot + 1, :], -1) for slot in range(slot_count)
    ]

    named = jnp.concatenate(named, axis=0).astype(jnp.float32)
    row = lax.broadcasted_iota(jnp.int32, (BUILD_ROWS, nodes), 0).astype(jnp.float32).astype(jnp.bfloat16)

    def build(block, carry):
        start = pl.multiple_of(block * BUILD_ROWS, BUILD_ROWS)
        shifted = (named - start.astype(jnp.float32)).astype(jnp.bfloat16)
        count = jnp.zeros((BUILD_ROWS, nodes), jnp.bfloat16)
        for slot in range(slot_count):
            count = jnp.where(row == shifted[slot : slot + 1, :], count + 1, count)
        table[pl.ds(start, BUILD_ROWS), :] = count
        return carry

    lax.fori_loop(0, total_rows // BUILD_ROWS, build, 0)

    share = 1.0 / degree_row.astype(jnp.float32)
    summed = dot(feat_t[...], table[:nodes, :])
    for fetch in fetches[4:]:
        fetch.wait()
    pre_self = dot_rows(w_self_ref[...], feat_t[...])
    w_neigh_t = jnp.transpose(w_neigh_ref[...])
    up_t = jnp.transpose(up_ref[...])

    inner_levels = inner.bit_length() - 1
    for low, high in ((0, inner_levels), (inner_levels, levels)):
        for level in range(low, high):
            row_copies[level].wait_recv()
        rows_t = jnp.concatenate([in_rows[level] for level in range(low, high)], axis=1)
        summed = summed + dot(rows_t, table[nodes + low * bnd : nodes + high * bnd, :])
    agg_t = (summed * share).astype(jnp.bfloat16)
    pre_sum = pre_self + dot(w_neigh_t, agg_t)
    sigmoid = jax.nn.sigmoid(pre_sum)
    pre_grad = (
        up_t.astype(jnp.float32) * sigmoid * (1.0 + pre_sum * (1.0 - sigmoid))
    ).astype(jnp.bfloat16)

    width = feat_t.shape[0]
    part_copies = []
    for half in range(2):
        left_t = feat_t[...] if half == 0 else agg_t
        stack[half] = dot_cols(left_t, pre_grad).astype(jnp.bfloat16)
        for mask in inner_masks:
            theirs = lax.rem(partner(me, mask), inner)
            copy = remote(
                stack.at[half, pl.ds(pl.multiple_of(theirs * chunk, chunk), chunk), :],
                part_in.at[half, mask], part_ss.at[half, mask], part_rs.at[half, mask], mask,
            )
            copy.start()
            part_copies.append(copy)

    slot_share = (dot(w_neigh_ref[...], pre_grad) * share).astype(jnp.bfloat16)
    out_grads[...] = dot_cols(table[nodes:, :], slot_share).astype(jnp.bfloat16)
    grad_copies = []

    def return_grads(level):
        span = pl.ds(level * bnd, bnd)
        copy = remote(
            out_grads.at[span, :], in_grads.at[span, :], grad_ss.at[level], grad_rs.at[level], 1 << level
        )
        copy.start()
        grad_copies.append(copy)

    for level in reversed(range(inner_levels, levels)):
        return_grads(level)
    hidden_ref[...] = jnp.transpose((pre_sum * sigmoid).astype(jnp.bfloat16))
    local = jnp.transpose(dot(w_self_ref[...], pre_grad)) + dot_cols(table[:nodes, :], slot_share)

    own = pl.ds(pl.multiple_of(mine * chunk, chunk), chunk)
    per_half = len(inner_masks)
    plane_copies = []
    for half in range(2):
        for copy in part_copies[half * per_half : (half + 1) * per_half]:
            copy.wait_recv()
        total = stack[half, own, :].astype(jnp.float32)
        for mask in inner_masks:
            total = total + part_in[half, mask].astype(jnp.float32)
        part[half] = total.astype(jnp.bfloat16)
        for mask in outer_masks:
            index = mask // inner
            copy = remote(
                part.at[half], plane_in.at[half, index],
                plane_ss.at[half, index], plane_rs.at[half, index], mask,
            )
            copy.start()
            plane_copies.append(copy)

    for level in reversed(range(inner_levels)):
        return_grads(level)

    per_outer = len(outer_masks)
    gather_copies = []
    for half in range(2):
        for copy in plane_copies[half * per_outer : (half + 1) * per_outer]:
            copy.wait_recv()
        terms = [part[half].astype(jnp.float32)]
        for index in range(1, outer):
            terms.append(plane_in[half, index].astype(jnp.float32))
        while len(terms) > 1:
            terms = [terms[i] + terms[i + 1] for i in range(0, len(terms), 2)]
        rows = pl.ds(pl.multiple_of(half * width + mine * chunk, chunk), chunk)
        gathered[rows, :] = terms[0].astype(jnp.bfloat16)
        for mask in inner_masks:
            copy = remote(
                gathered.at[rows, :], gathered.at[rows, :],
                gather_ss.at[half, mask], gather_rs.at[half, mask], mask,
            )
            copy.start()
            gather_copies.append(copy)

    for copy in grad_copies:
        copy.wait_recv()
    node_ref[...] = (local + dot(pick[...], in_grads[...])).astype(jnp.bfloat16)
    for copy in row_copies + part_copies + grad_copies + plane_copies:
        copy.wait_send()
    for copy in gather_copies:
        copy.wait_send()
    for copy in gather_copies:
        copy.wait_recv()


def finish(hidden, node, gathered, hidden_hbm, node_hbm, step_hbm, step, sems):
    copies = [
        pltpu.make_async_copy(hidden, hidden_hbm, sems.at[0]),
        pltpu.make_async_copy(node, node_hbm, sems.at[1]),
        pltpu.make_async_copy(step, step_hbm, sems.at[2]),
    ]
    copies[0].start()
    copies[1].start()
    whole = gathered[...].astype(jnp.float32)
    step[...] = whole * lax.rsqrt(jnp.mean(whole * whole) + epsilon)
    copies[2].start()
    for copy in copies:
        copy.wait()


def per_device(features, w_self, w_neigh, neighbors, degree, boundary, upstream):
    size = lax.axis_size("dom")
    levels = size.bit_length() - 1
    inner = min(size, 1 << INNER_BITS)
    outer = size // inner
    nodes, width = features.shape
    bnd = boundary.shape[2]
    rows = levels * bnd
    chunk = width // inner
    bf16 = jnp.bfloat16
    sem = pltpu.SemaphoreType.DMA
    vmem = pl.BlockSpec(memory_space=pltpu.VMEM)
    hbm = pl.BlockSpec(memory_space=pltpu.HBM)
    args = (features, w_self, w_neigh, neighbors.T, degree, boundary.transpose(1, 0, 2), upstream)
    args = tuple(pltpu.with_memory_space_constraint(arg, pltpu.HBM) for arg in args)
    hidden, node, gathered = pl.pallas_call(
        functools.partial(kernel, inner, outer, levels, bnd),
        out_shape=(
            pltpu.VMEM((nodes, width), bf16),
            pltpu.VMEM((nodes, width), bf16),
            pltpu.VMEM((2 * width, width), bf16),
        ),
        in_specs=[hbm] * 7,
        out_specs=(vmem, vmem, vmem),
        scratch_shapes=[pltpu.VMEM(arg.shape, arg.dtype) for arg in args] + [
            sem((7,)),
            pltpu.VMEM((width, nodes), bf16),
            pltpu.VMEM((nodes + rows, nodes), bf16),
            pltpu.VMEM((nodes, rows), bf16),
            pltpu.VMEM((levels, width, bnd), bf16),
            pltpu.VMEM((levels, width, bnd), bf16),
            pltpu.VMEM((rows, width), bf16),
            pltpu.VMEM((rows, width), bf16),
            pltpu.VMEM((2, width, width), bf16),
            pltpu.VMEM((2, inner, chunk, width), bf16),
            pltpu.VMEM((2, chunk, width), bf16),
            pltpu.VMEM((2, outer, chunk, width), bf16),
            sem((levels,)), sem((levels,)), sem((levels,)), sem((levels,)),
            sem((2, inner)), sem((2, inner)), sem((2, outer)), sem((2, outer)), sem((2, inner)), sem((2, inner)),
        ],
        compiler_params=pltpu.CompilerParams(
            collective_id=0, has_side_effects=True, vmem_limit_bytes=40 << 20
        ),
        cost_estimate=pl.CostEstimate(flops=1 << 30, bytes_accessed=3 << 20, transcendentals=nodes * width),
    )(*args)
    return pl.pallas_call(
        finish,
        out_shape=(
            jax.ShapeDtypeStruct((nodes, width), bf16),
            jax.ShapeDtypeStruct((nodes, width), bf16),
            jax.ShapeDtypeStruct((2 * width, width), jnp.float32),
        ),
        in_specs=[vmem] * 3,
        out_specs=(hbm, hbm, hbm),
        scratch_shapes=[pltpu.VMEM((2 * width, width), jnp.float32), sem((3,))],
        compiler_params=pltpu.CompilerParams(vmem_limit_bytes=16 << 20),
        cost_estimate=pl.CostEstimate(flops=1 << 18, bytes_accessed=1 << 20, transcendentals=0),
    )(hidden, node, gathered)


def solution(mesh):
    return jax.shard_map(
        per_device,
        mesh=mesh,
        in_specs=(
            P("dom", None),
            P(),
            P(),
            P("dom", None),
            P("dom"),
            P("dom", None, None),
            P("dom", None),
        ),
        out_specs=(P("dom", None), P("dom", None), P()),
        check_vma=False,
    )
```

```python
import functools

import jax
import jax.numpy as jnp
from jax import lax
from jax.experimental import pallas as pl
from jax.experimental.pallas import tpu as pltpu
from jax.sharding import PartitionSpec as P

epsilon = 1e-06
INNER_BITS = 3
BUILD_ROWS = 128


def partner(me, mask):
    other = me
    bit = 0
    while mask >> bit:
        if (mask >> bit) & 1:
            size = 1 << bit
            other = other + size * (1 - 2 * lax.rem(lax.div(me, size), 2))
        bit += 1
    return other


def dot(a, b):
    return jnp.dot(a, b, preferred_element_type=jnp.float32)


def dot_rows(a, b):
    return lax.dot_general(a, b, (((0,), (0,)), ((), ())), preferred_element_type=jnp.float32)


def dot_cols(a, b):
    return lax.dot_general(a, b, (((1,), (1,)), ((), ())), preferred_element_type=jnp.float32)


def kernel(
    inner, outer, levels, bnd,
    feat_hbm, w_self_hbm, w_neigh_hbm, slots_hbm, degree_hbm, boundary_hbm, up_hbm,
    hidden_ref, node_ref, gathered,
    feat_ref, w_self_ref, w_neigh_ref, slots_ref, degree_ref, boundary_ref, up_ref, fetch_sem,
    feat_t, table, pick, out_rows, in_rows, out_grads, in_grads,
    stack, pair_in, paired, part_in, part, plane_in,
    pair_ss, pair_rs, row_ss, row_rs, grad_ss, grad_rs, part_ss, part_rs, plane_ss, plane_rs, gather_ss, gather_rs,
):
    me = lax.axis_index("dom")
    nodes = feat_ref.shape[0]
    slot_count = slots_ref.shape[0]
    total_rows = table.shape[0]
    chunk = stack.shape[1] // inner
    mine = lax.rem(me, inner)

    fetches = [
        pltpu.make_async_copy(src, dst, fetch_sem.at[index])
        for index, (src, dst) in enumerate((
            (boundary_hbm, boundary_ref), (feat_hbm, feat_ref), (degree_hbm, degree_ref),
            (slots_hbm, slots_ref), (w_self_hbm, w_self_ref), (w_neigh_hbm, w_neigh_ref),
            (up_hbm, up_ref),
        ))
    ]
    for fetch in fetches:
        fetch.start()

    inner_masks = list(range(inner - 1, 0, -1))
    outer_masks = [e * inner for e in range(outer - 1, 0, -1)]
    barrier = pltpu.get_barrier_semaphore()
    greeted = [1 << level for level in range(levels)]
    greeted += [mask for mask in inner_masks + outer_masks if mask.bit_count() > 2]
    for mask in greeted:
        pl.semaphore_signal(
            barrier, inc=1, device_id=(partner(me, mask),), device_id_type=pl.DeviceIdType.MESH
        )

    def remote(src, dst, send_sem, recv_sem, mask):
        return pltpu.make_async_remote_copy(
            src_ref=src, dst_ref=dst, send_sem=send_sem, recv_sem=recv_sem,
            device_id=(partner(me, mask),), device_id_type=pl.DeviceIdType.MESH,
        )

    fetches[0].wait()
    fetches[1].wait()
    feat_t[...] = jnp.transpose(feat_ref[...])

    row_id = lax.broadcasted_iota(jnp.int32, (nodes, bnd), 0)
    for level in range(levels):
        hot = (row_id == boundary_ref[level]).astype(jnp.float32).astype(jnp.bfloat16)
        pick[:, pl.ds(level * bnd, bnd)] = hot
    picked = dot(feat_t[...], pick[...]).astype(jnp.bfloat16)
    for level in range(levels):
        out_rows[level] = picked[:, level * bnd : (level + 1) * bnd]
    pl.semaphore_wait(barrier, len(greeted))
    row_copies = [
        remote(out_rows.at[level], in_rows.at[level], row_ss.at[level], row_rs.at[level], 1 << level)
        for level in range(levels)
    ]
    for copy in reversed(row_copies):
        copy.start()

    fetches[2].wait()
    fetches[3].wait()
    degree_row = degree_ref[...].reshape(1, nodes)
    named = [
        jnp.where(degree_row > slot, slots_ref[slot : slot + 1, :], -1) for slot in range(slot_count)
    ]

    named = jnp.concatenate(named, axis=0).astype(jnp.float32)
    row = lax.broadcasted_iota(jnp.int32, (BUILD_ROWS, nodes), 0).astype(jnp.float32).astype(jnp.bfloat16)

    def build(block, carry):
        start = pl.multiple_of(block * BUILD_ROWS, BUILD_ROWS)
        shifted = (named - start.astype(jnp.float32)).astype(jnp.bfloat16)
        count = jnp.zeros((BUILD_ROWS, nodes), jnp.bfloat16)
        for slot in range(slot_count):
            count = jnp.where(row == shifted[slot : slot + 1, :], count + 1, count)
        table[pl.ds(start, BUILD_ROWS), :] = count
        return carry

    lax.fori_loop(0, total_rows // BUILD_ROWS, build, 0)

    share = 1.0 / degree_row.astype(jnp.float32)
    summed = dot(feat_t[...], table[:nodes, :])
    for fetch in fetches[4:]:
        fetch.wait()
    pre_self = dot_rows(w_self_ref[...], feat_t[...])
    w_neigh_t = jnp.transpose(w_neigh_ref[...])
    up_t = jnp.transpose(up_ref[...])

    inner_levels = inner.bit_length() - 1
    for low, high in ((0, inner_levels), (inner_levels, levels)):
        for level in range(low, high):
            row_copies[level].wait_recv()
        rows_t = jnp.concatenate([in_rows[level] for level in range(low, high)], axis=1)
        summed = summed + dot(rows_t, table[nodes + low * bnd : nodes + high * bnd, :])
    agg_t = (summed * share).astype(jnp.bfloat16)
    pre_sum = pre_self + dot(w_neigh_t, agg_t)
    sigmoid = jax.nn.sigmoid(pre_sum)
    pre_grad = (
        up_t.astype(jnp.float32) * sigmoid * (1.0 + pre_sum * (1.0 - sigmoid))
    ).astype(jnp.bfloat16)

    width = feat_t.shape[0]
    core = lax.rem(me, 2)
    stack[0] = dot_cols(feat_t[...], pre_grad).astype(jnp.bfloat16)
    stack[1] = dot_cols(agg_t, pre_grad).astype(jnp.bfloat16)
    pair_copy = remote(stack.at[1 - core], pair_in, pair_ss.at[0], pair_rs.at[0], 1)
    pair_copy.start()

    slot_share = (dot(w_neigh_ref[...], pre_grad) * share).astype(jnp.bfloat16)
    out_grads[...] = dot_cols(table[nodes:, :], slot_share).astype(jnp.bfloat16)
    grad_copies = []

    def return_grads(level):
        span = pl.ds(level * bnd, bnd)
        copy = remote(
            out_grads.at[span, :], in_grads.at[span, :], grad_ss.at[level], grad_rs.at[level], 1 << level
        )
        copy.start()
        grad_copies.append(copy)

    for level in reversed(range(inner_levels, levels)):
        return_grads(level)
    pair_copy.wait_recv()
    paired[...] = (stack[core].astype(jnp.float32) + pair_in[...].astype(jnp.float32)).astype(jnp.bfloat16)
    chip_masks = [mask for mask in inner_masks if mask % 2 == 0]
    part_copies = []
    for half in range(2):
        for mask in chip_masks:
            theirs = lax.div(lax.rem(partner(me, mask), inner), 2) * (2 * chunk) + half * chunk
            copy = remote(
                paired.at[pl.ds(pl.multiple_of(theirs, chunk), chunk), :],
                part_in.at[half, mask], part_ss.at[half, mask], part_rs.at[half, mask], mask,
            )
            copy.start()
            part_copies.append(copy)

    hidden_ref[...] = jnp.transpose((pre_sum * sigmoid).astype(jnp.bfloat16))
    local = jnp.transpose(dot(w_self_ref[...], pre_grad)) + dot_cols(table[:nodes, :], slot_share)

    first = lax.div(mine, 2) * (2 * chunk)
    per_half = len(chip_masks)
    plane_copies = []
    for half in range(2):
        for copy in part_copies[half * per_half : (half + 1) * per_half]:
            copy.wait_recv()
        own = pl.ds(pl.multiple_of(first + half * chunk, chunk), chunk)
        total = paired[own, :].astype(jnp.float32)
        for mask in chip_masks:
            total = total + part_in[half, mask].astype(jnp.float32)
        part[half] = total.astype(jnp.bfloat16)
        for mask in outer_masks:
            index = mask // inner
            copy = remote(
                part.at[half], plane_in.at[half, index],
                plane_ss.at[half, index], plane_rs.at[half, index], mask,
            )
            copy.start()
            plane_copies.append(copy)

    for level in reversed(range(inner_levels)):
        return_grads(level)

    per_outer = len(outer_masks)
    gather_copies = []
    for half in range(2):
        for copy in plane_copies[half * per_outer : (half + 1) * per_outer]:
            copy.wait_recv()
        terms = [part[half].astype(jnp.float32)]
        for index in range(1, outer):
            terms.append(plane_in[half, index].astype(jnp.float32))
        while len(terms) > 1:
            terms = [terms[i] + terms[i + 1] for i in range(0, len(terms), 2)]
        rows = pl.ds(pl.multiple_of(core * width + first + half * chunk, chunk), chunk)
        gathered[rows, :] = terms[0].astype(jnp.bfloat16)
        for mask in inner_masks:
            copy = remote(
                gathered.at[rows, :], gathered.at[rows, :],
                gather_ss.at[half, mask], gather_rs.at[half, mask], mask,
            )
            copy.start()
            gather_copies.append(copy)

    for copy in grad_copies:
        copy.wait_recv()
    node_ref[...] = (local + dot(pick[...], in_grads[...])).astype(jnp.bfloat16)
    for copy in gather_copies:
        copy.wait_recv()

    for copy in [pair_copy] + row_copies + part_copies + grad_copies + plane_copies + gather_copies:
        copy.wait_send()


def finish(hidden, node, gathered, hidden_hbm, node_hbm, step_hbm, step, sems):
    copies = [
        pltpu.make_async_copy(hidden, hidden_hbm, sems.at[0]),
        pltpu.make_async_copy(node, node_hbm, sems.at[1]),
        pltpu.make_async_copy(step, step_hbm, sems.at[2]),
    ]
    copies[0].start()
    copies[1].start()
    whole = gathered[...].astype(jnp.float32)
    step[...] = whole * lax.rsqrt(jnp.mean(whole * whole) + epsilon)
    copies[2].start()
    for copy in copies:
        copy.wait()


def per_device(features, w_self, w_neigh, neighbors, degree, boundary, upstream):
    size = lax.axis_size("dom")
    levels = size.bit_length() - 1
    inner = min(size, 1 << INNER_BITS)
    outer = size // inner
    nodes, width = features.shape
    bnd = boundary.shape[2]
    rows = levels * bnd
    chunk = width // inner
    bf16 = jnp.bfloat16
    sem = pltpu.SemaphoreType.DMA
    vmem = pl.BlockSpec(memory_space=pltpu.VMEM)
    hbm = pl.BlockSpec(memory_space=pltpu.HBM)
    args = (features, w_self, w_neigh, neighbors.T, degree, boundary.transpose(1, 0, 2), upstream)
    args = tuple(pltpu.with_memory_space_constraint(arg, pltpu.HBM) for arg in args)
    hidden, node, gathered = pl.pallas_call(
        functools.partial(kernel, inner, outer, levels, bnd),
        out_shape=(
            pltpu.VMEM((nodes, width), bf16),
            pltpu.VMEM((nodes, width), bf16),
            pltpu.VMEM((2 * width, width), bf16),
        ),
        in_specs=[hbm] * 7,
        out_specs=(vmem, vmem, vmem),
        scratch_shapes=[pltpu.VMEM(arg.shape, arg.dtype) for arg in args] + [
            sem((7,)),
            pltpu.VMEM((width, nodes), bf16),
            pltpu.VMEM((nodes + rows, nodes), bf16),
            pltpu.VMEM((nodes, rows), bf16),
            pltpu.VMEM((levels, width, bnd), bf16),
            pltpu.VMEM((levels, width, bnd), bf16),
            pltpu.VMEM((rows, width), bf16),
            pltpu.VMEM((rows, width), bf16),
            pltpu.VMEM((2, width, width), bf16),
            pltpu.VMEM((width, width), bf16),
            pltpu.VMEM((width, width), bf16),
            pltpu.VMEM((2, inner, chunk, width), bf16),
            pltpu.VMEM((2, chunk, width), bf16),
            pltpu.VMEM((2, outer, chunk, width), bf16),
            sem((1,)), sem((1,)), sem((levels,)), sem((levels,)), sem((levels,)), sem((levels,)),
            sem((2, inner)), sem((2, inner)), sem((2, outer)), sem((2, outer)), sem((2, inner)), sem((2, inner)),
        ],
        compiler_params=pltpu.CompilerParams(
            collective_id=0, has_side_effects=True, vmem_limit_bytes=40 << 20
        ),
        cost_estimate=pl.CostEstimate(flops=1 << 30, bytes_accessed=3 << 20, transcendentals=nodes * width),
    )(*args)
    return pl.pallas_call(
        finish,
        out_shape=(
            jax.ShapeDtypeStruct((nodes, width), bf16),
            jax.ShapeDtypeStruct((nodes, width), bf16),
            jax.ShapeDtypeStruct((2 * width, width), jnp.float32),
        ),
        in_specs=[vmem] * 3,
        out_specs=(hbm, hbm, hbm),
        scratch_shapes=[pltpu.VMEM((2 * width, width), jnp.float32), sem((3,))],
        compiler_params=pltpu.CompilerParams(vmem_limit_bytes=16 << 20),
        cost_estimate=pl.CostEstimate(flops=1 << 18, bytes_accessed=1 << 20, transcendentals=0),
    )(hidden, node, gathered)


def solution(mesh):
    return jax.shard_map(
        per_device,
        mesh=mesh,
        in_specs=(
            P("dom", None),
            P(),
            P(),
            P("dom", None),
            P("dom"),
            P("dom", None, None),
            P("dom", None),
        ),
        out_specs=(P("dom", None), P("dom", None), P()),
        check_vma=False,
    )
```

```python
import functools

import jax
import jax.numpy as jnp
from jax import lax
from jax.experimental import pallas as pl
from jax.experimental.pallas import tpu as pltpu
from jax.sharding import PartitionSpec as P

epsilon = 1e-06
INNER_BITS = 3
BUILD_ROWS = 128
FORWARD_NODES = 256


def partner(me, mask):
    other = me
    bit = 0
    while mask >> bit:
        if (mask >> bit) & 1:
            size = 1 << bit
            other = other + size * (1 - 2 * lax.rem(lax.div(me, size), 2))
        bit += 1
    return other


def dot(a, b):
    return jnp.dot(a, b, preferred_element_type=jnp.float32)


def dot_rows(a, b):
    return lax.dot_general(a, b, (((0,), (0,)), ((), ())), preferred_element_type=jnp.float32)


def dot_cols(a, b):
    return lax.dot_general(a, b, (((1,), (1,)), ((), ())), preferred_element_type=jnp.float32)


def kernel(
    inner, outer, levels, bnd,
    feat_hbm, w_self_hbm, w_neigh_hbm, slots_hbm, degree_hbm, boundary_hbm, up_hbm,
    hidden_ref, node_ref, gathered,
    feat_ref, w_self_ref, w_neigh_ref, slots_ref, degree_ref, boundary_ref, up_ref, fetch_sem,
    lefts, summed, pre_ref, hidden_t, pre_grad_ref, up_t, w_neigh_t, share_ref, table, pick, out_rows, in_rows, out_grads, in_grads,
    stack, part_in, part, plane_in,
    row_ss, row_rs, grad_ss, grad_rs, part_ss, part_rs, plane_ss, plane_rs, gather_ss, gather_rs,
):
    me = lax.axis_index("dom")
    nodes = feat_ref.shape[0]
    slot_count = slots_ref.shape[0]
    total_rows = table.shape[0]
    chunk = stack.shape[1] // inner
    mine = lax.rem(me, inner)

    fetches = [
        pltpu.make_async_copy(src, dst, fetch_sem.at[index])
        for index, (src, dst) in enumerate((
            (boundary_hbm, boundary_ref), (feat_hbm, feat_ref), (degree_hbm, degree_ref),
            (slots_hbm, slots_ref), (w_self_hbm, w_self_ref), (w_neigh_hbm, w_neigh_ref),
            (up_hbm, up_ref),
        ))
    ]
    for fetch in fetches:
        fetch.start()

    inner_masks = list(range(inner - 1, 0, -1))
    outer_masks = [e * inner for e in range(outer - 1, 0, -1)]
    barrier = pltpu.get_barrier_semaphore()
    greeted = [1 << level for level in range(levels)]
    greeted += [mask for mask in inner_masks + outer_masks if mask.bit_count() > 2]
    for mask in greeted:
        pl.semaphore_signal(
            barrier, inc=1, device_id=(partner(me, mask),), device_id_type=pl.DeviceIdType.MESH
        )

    def remote(src, dst, send_sem, recv_sem, mask):
        return pltpu.make_async_remote_copy(
            src_ref=src, dst_ref=dst, send_sem=send_sem, recv_sem=recv_sem,
            device_id=(partner(me, mask),), device_id_type=pl.DeviceIdType.MESH,
        )

    fetches[0].wait()
    fetches[1].wait()
    lefts[0] = jnp.transpose(feat_ref[...])

    row_id = lax.broadcasted_iota(jnp.int32, (nodes, bnd), 0)
    for level in range(levels):
        hot = (row_id == boundary_ref[level]).astype(jnp.float32).astype(jnp.bfloat16)
        pick[:, pl.ds(level * bnd, bnd)] = hot
    picked = dot(lefts[0], pick[...]).astype(jnp.bfloat16)
    for level in range(levels):
        out_rows[level] = picked[:, level * bnd : (level + 1) * bnd]
    pl.semaphore_wait(barrier, len(greeted))
    row_copies = [
        remote(out_rows.at[level], in_rows.at[level], row_ss.at[level], row_rs.at[level], 1 << level)
        for level in range(levels)
    ]
    for copy in reversed(row_copies):
        copy.start()

    fetches[2].wait()
    fetches[3].wait()
    degree_row = degree_ref[...].reshape(1, nodes)
    named = [
        jnp.where(degree_row > slot, slots_ref[slot : slot + 1, :], -1) for slot in range(slot_count)
    ]

    named = jnp.concatenate(named, axis=0).astype(jnp.float32)
    row = lax.broadcasted_iota(jnp.int32, (BUILD_ROWS, nodes), 0).astype(jnp.float32).astype(jnp.bfloat16)

    def build(block, carry):
        start = pl.multiple_of(block * BUILD_ROWS, BUILD_ROWS)
        shifted = (named - start.astype(jnp.float32)).astype(jnp.bfloat16)
        count = jnp.zeros((BUILD_ROWS, nodes), jnp.bfloat16)
        for slot in range(slot_count):
            count = jnp.where(row == shifted[slot : slot + 1, :], count + 1, count)
        table[pl.ds(start, BUILD_ROWS), :] = count
        return carry

    lax.fori_loop(0, total_rows // BUILD_ROWS, build, 0)

    share_ref[...] = 1.0 / degree_row.astype(jnp.float32)
    for fetch in fetches[4:]:
        fetch.wait()
    w_neigh_t[...] = jnp.transpose(w_neigh_ref[...])
    up_t[...] = jnp.transpose(up_ref[...])

    def ahead(block, carry):
        span = pl.ds(pl.multiple_of(block * FORWARD_NODES, FORWARD_NODES), FORWARD_NODES)
        summed[:, span] = dot(lefts[0], table[:nodes, span])
        pre_ref[:, span] = dot_rows(w_self_ref[...], lefts[0, :, span])
        return carry

    lax.fori_loop(0, nodes // FORWARD_NODES, ahead, 0)
    for copy in row_copies:
        copy.wait_recv()

    def forward(block, carry):
        span = pl.ds(pl.multiple_of(block * FORWARD_NODES, FORWARD_NODES), FORWARD_NODES)
        rows_t = jnp.concatenate([in_rows[level] for level in range(levels)], axis=1)
        agg = summed[:, span] + dot(rows_t, table[nodes:, span])
        agg = (agg * share_ref[:, span]).astype(jnp.bfloat16)
        lefts[1, :, span] = agg
        pre_sum = pre_ref[:, span] + dot(w_neigh_t[...], agg)
        sigmoid = jax.nn.sigmoid(pre_sum)
        hidden_t[:, span] = (pre_sum * sigmoid).astype(jnp.bfloat16)
        pre_grad_ref[:, span] = (
            up_t[:, span].astype(jnp.float32) * sigmoid * (1.0 + pre_sum * (1.0 - sigmoid))
        ).astype(jnp.bfloat16)
        return carry

    lax.fori_loop(0, nodes // FORWARD_NODES, forward, 0)

    width = lefts.shape[1]
    inner_levels = inner.bit_length() - 1

    def part_copy(half, mask):
        theirs = lax.rem(partner(me, mask), inner)
        return remote(
            stack.at[half, pl.ds(pl.multiple_of(theirs * chunk, chunk), chunk), :],
            part_in.at[half, mask], part_ss.at[half, mask], part_rs.at[half, mask], mask,
        )

    def plane_copy(half, mask):
        index = mask // inner
        return remote(
            part.at[half], plane_in.at[half, index],
            plane_ss.at[half, index], plane_rs.at[half, index], mask,
        )

    def gather_copy(half, mask):
        rows = pl.ds(pl.multiple_of(half * width + mine * chunk, chunk), chunk)
        return remote(
            gathered.at[rows, :], gathered.at[rows, :],
            gather_ss.at[half, mask], gather_rs.at[half, mask], mask,
        )

    def send_parts(half, carry):
        stack[half] = dot_cols(lefts[half], pre_grad_ref[...]).astype(jnp.bfloat16)
        for mask in inner_masks:
            part_copy(half, mask).start()
        return carry

    lax.fori_loop(0, 2, send_parts, 0)

    pre_grad = pre_grad_ref[...]
    share = share_ref[...]
    slot_share = (dot(w_neigh_ref[...], pre_grad) * share).astype(jnp.bfloat16)
    out_grads[...] = dot_cols(table[nodes:, :], slot_share).astype(jnp.bfloat16)
    grad_copies = []

    def return_grads(level):
        span = pl.ds(level * bnd, bnd)
        copy = remote(
            out_grads.at[span, :], in_grads.at[span, :], grad_ss.at[level], grad_rs.at[level], 1 << level
        )
        copy.start()
        grad_copies.append(copy)

    for level in reversed(range(inner_levels, levels)):
        return_grads(level)
    hidden_ref[...] = jnp.transpose(hidden_t[...])
    local = jnp.transpose(dot(w_self_ref[...], pre_grad)) + dot_cols(table[:nodes, :], slot_share)

    own = pl.ds(pl.multiple_of(mine * chunk, chunk), chunk)
    def send_planes(half, carry):
        for mask in inner_masks:
            part_copy(half, mask).wait_recv()
        total = stack[half, own, :].astype(jnp.float32)
        for mask in inner_masks:
            total = total + part_in[half, mask].astype(jnp.float32)
        part[half] = total.astype(jnp.bfloat16)
        for mask in outer_masks:
            plane_copy(half, mask).start()
        return carry

    lax.fori_loop(0, 2, send_planes, 0)
    for level in reversed(range(inner_levels)):
        return_grads(level)

    def send_gathers(half, carry):
        for mask in outer_masks:
            plane_copy(half, mask).wait_recv()
        terms = [part[half].astype(jnp.float32)]
        for index in range(1, outer):
            terms.append(plane_in[half, index].astype(jnp.float32))
        while len(terms) > 1:
            terms = [terms[i] + terms[i + 1] for i in range(0, len(terms), 2)]
        rows = pl.ds(pl.multiple_of(half * width + mine * chunk, chunk), chunk)
        gathered[rows, :] = terms[0].astype(jnp.bfloat16)
        for mask in inner_masks:
            gather_copy(half, mask).start()
        return carry

    lax.fori_loop(0, 2, send_gathers, 0)

    for copy in grad_copies:
        copy.wait_recv()
    node_ref[...] = (local + dot(pick[...], in_grads[...])).astype(jnp.bfloat16)

    def settle(half, carry):
        for mask in inner_masks:
            part_copy(half, mask).wait_send()
            gather_copy(half, mask).wait()
        for mask in outer_masks:
            plane_copy(half, mask).wait_send()
        return carry

    lax.fori_loop(0, 2, settle, 0)
    for copy in row_copies + grad_copies:
        copy.wait_send()


def finish(hidden, node, gathered, hidden_hbm, node_hbm, step_hbm, step, sems):
    copies = [
        pltpu.make_async_copy(hidden, hidden_hbm, sems.at[0]),
        pltpu.make_async_copy(node, node_hbm, sems.at[1]),
        pltpu.make_async_copy(step, step_hbm, sems.at[2]),
    ]
    copies[0].start()
    copies[1].start()
    whole = gathered[...].astype(jnp.float32)
    step[...] = whole * lax.rsqrt(jnp.mean(whole * whole) + epsilon)
    copies[2].start()
    for copy in copies:
        copy.wait()


def per_device(features, w_self, w_neigh, neighbors, degree, boundary, upstream):
    size = lax.axis_size("dom")
    levels = size.bit_length() - 1
    inner = min(size, 1 << INNER_BITS)
    outer = size // inner
    nodes, width = features.shape
    bnd = boundary.shape[2]
    rows = levels * bnd
    chunk = width // inner
    bf16 = jnp.bfloat16
    sem = pltpu.SemaphoreType.DMA
    vmem = pl.BlockSpec(memory_space=pltpu.VMEM)
    hbm = pl.BlockSpec(memory_space=pltpu.HBM)
    args = (features, w_self, w_neigh, neighbors.T, degree, boundary.transpose(1, 0, 2), upstream)
    args = tuple(pltpu.with_memory_space_constraint(arg, pltpu.HBM) for arg in args)
    hidden, node, gathered = pl.pallas_call(
        functools.partial(kernel, inner, outer, levels, bnd),
        out_shape=(
            pltpu.VMEM((nodes, width), bf16),
            pltpu.VMEM((nodes, width), bf16),
            pltpu.VMEM((2 * width, width), bf16),
        ),
        in_specs=[hbm] * 7,
        out_specs=(vmem, vmem, vmem),
        scratch_shapes=[pltpu.VMEM(arg.shape, arg.dtype) for arg in args] + [
            sem((7,)),
            pltpu.VMEM((2, width, nodes), bf16),
            pltpu.VMEM((width, nodes), jnp.float32),
            pltpu.VMEM((width, nodes), jnp.float32),
            pltpu.VMEM((width, nodes), bf16),
            pltpu.VMEM((width, nodes), bf16),
            pltpu.VMEM((width, nodes), bf16),
            pltpu.VMEM((width, width), bf16),
            pltpu.VMEM((1, nodes), jnp.float32),
            pltpu.VMEM((nodes + rows, nodes), bf16),
            pltpu.VMEM((nodes, rows), bf16),
            pltpu.VMEM((levels, width, bnd), bf16),
            pltpu.VMEM((levels, width, bnd), bf16),
            pltpu.VMEM((rows, width), bf16),
            pltpu.VMEM((rows, width), bf16),
            pltpu.VMEM((2, width, width), bf16),
            pltpu.VMEM((2, inner, chunk, width), bf16),
            pltpu.VMEM((2, chunk, width), bf16),
            pltpu.VMEM((2, outer, chunk, width), bf16),
            sem((levels,)), sem((levels,)), sem((levels,)), sem((levels,)),
            sem((2, inner)), sem((2, inner)), sem((2, outer)), sem((2, outer)), sem((2, inner)), sem((2, inner)),
        ],
        compiler_params=pltpu.CompilerParams(
            collective_id=0, has_side_effects=True, vmem_limit_bytes=40 << 20
        ),
        cost_estimate=pl.CostEstimate(flops=1 << 30, bytes_accessed=3 << 20, transcendentals=nodes * width),
    )(*args)
    return pl.pallas_call(
        finish,
        out_shape=(
            jax.ShapeDtypeStruct((nodes, width), bf16),
            jax.ShapeDtypeStruct((nodes, width), bf16),
            jax.ShapeDtypeStruct((2 * width, width), jnp.float32),
        ),
        in_specs=[vmem] * 3,
        out_specs=(hbm, hbm, hbm),
        scratch_shapes=[pltpu.VMEM((2 * width, width), jnp.float32), sem((3,))],
        compiler_params=pltpu.CompilerParams(vmem_limit_bytes=16 << 20),
        cost_estimate=pl.CostEstimate(flops=1 << 18, bytes_accessed=1 << 20, transcendentals=0),
    )(hidden, node, gathered)


def solution(mesh):
    return jax.shard_map(
        per_device,
        mesh=mesh,
        in_specs=(
            P("dom", None),
            P(),
            P(),
            P("dom", None),
            P("dom"),
            P("dom", None, None),
            P("dom", None),
        ),
        out_specs=(P("dom", None), P("dom", None), P()),
        check_vma=False,
    )
```
